32 devices in a mesh: dp: 8 (over y, x, core), mlp: 4 (over z).
Axes of the slice: x: 2, y: 2, z: 4, core: 2. Of those that a mesh axis runs over, the one named last changes fastest.
Arguments:
- tokens: bfloat16 [32768, 1024], P(('dp', 'mlp')), may hold values from -6 to 6
- gain: float32 [1024], replicated, may hold values from 0.5 to 1.5
- bias: float32 [1024], replicated, may hold values from -1.5 to 1.5
- w_qkv: bfloat16 [1024, 3072], replicated, may hold values from -0.1875 to 0.1875
- w_out: bfloat16 [1024, 1024], replicated, may hold values from -1.5 to 1.5
- w_up: bfloat16 [1024, 4096], P(None, 'mlp'), may hold values from -0.1875 to 0.1875
- w_down: bfloat16 [4096, 1024], P('mlp'), may hold values from -0.09375 to 0.09375
- lengths: int32 [32, 8], P(('dp', 'mlp')), may hold values from 1 to 512, 1024 in all within a row
- grad_out: bfloat16 [32768, 1024], P(('dp', 'mlp')), may hold values from -6 to 6
Outputs:
- result: bfloat16 [32768, 1024], P(('dp', 'mlp'))
- d_tokens: float32 [32768, 1024], P(('dp', 'mlp'))
- d_gain: float32 [1024], replicated
- d_bias: float32 [1024], replicated
- d_qkv: float32 [1024, 3072], replicated
- d_out: float32 [1024, 1024], replicated
- d_up: float32 [1024, 4096], P('dp', 'mlp')
- d_down: float32 [4096, 1024], P('mlp', 'dp')
The draws below stay inside these ranges and needn't reach their ends.
Inputs may be any that keep to these rules, and one draw needn't show every extreme that they name: Each row's 8 document lengths sum to 1024, and one of them is exactly 512.
All inputs are finite; a program needn't handle non-finite values.
Results may differ from the reference program's by a relative error of at most 0.0086.
Values may be sent and summed in bfloat16 or wider, within the bound.
A program may use at most 384 MiB of HBM per device.

```python
import math
import jax
import jax.numpy as jnp
import numpy as np
from jax import lax

D = 1024
H = 16
HD = 64
ROT = 16
FF = 4096
ROW = 1024
NDOC = 8
MOST = 512
ROWS = 32
TOKENS = 32768


def strengthened(array, key, source, target, blocks, factor):
    owner, partner = [(jnp.arange(array.shape[dim]) // (array.shape[dim] // blocks)).reshape([-1 if axis == dim else 1 for axis in range(array.ndim)]) for dim in (source, target)]
    chosen = jax.random.permutation(key, blocks)[partner]
    strong = (owner == chosen) | (owner == (partner + blocks // 2) % blocks)
    return jnp.where(strong, factor * array, array)


def block_levels(key, shape, cuts, low, largest):
    def one(position, blocks):
        heights = jax.random.uniform(jax.random.fold_in(jax.random.fold_in(key, 6), position), (blocks,), jnp.float32, low / len(cuts), largest / len(cuts))
        return jnp.repeat(jnp.exp(heights), shape[position] // blocks).reshape((-1,) + (1,) * (len(shape) - position - 1))

    level = one(*cuts[0])
    for cut in cuts[1:]:
        level = level * one(*cut)
    return level


def profile(count, total, bound, lean):
    loads = [(1 << 20) // math.isqrt(grade ** lean) + 1 for grade in range(2, count + 1)]
    surplus, counts = total - bound - (count - 1), [1] * (count - 1)
    while surplus > 0:
        free = [i for i in range(count - 1) if counts[i] < bound]
        pool, budget = sum([loads[i] for i in free]), surplus
        for i in free:
            extra = min(bound - counts[i], max(1, budget * loads[i] // pool), surplus)
            counts[i] = counts[i] + extra
            surplus = surplus - extra
    return np.array([bound] + counts)


def uneven(own_key, count, total, most, lean):
    if count == 2:
        one = jax.random.randint(own_key, (), max(1, total - most), min(most, total - 1) + 1)
        return jnp.stack([one, total - one])
    sizes = jnp.asarray(profile(count, total, most, lean), jnp.int32)
    couples = (count - 1) // 2
    giver, receiver = sizes[1:1 + 2 * couples:2], sizes[2:2 + 2 * couples:2]
    room = jnp.minimum(giver - 1, most - receiver)
    moved = jax.random.randint(jax.random.fold_in(own_key, 1), (couples,), 0, 1 << 20) % (room + 1)
    sizes = sizes.at[1:1 + 2 * couples:2].set(giver - moved).at[2:2 + 2 * couples:2].set(receiver + moved)
    return sizes[jax.random.permutation(jax.random.fold_in(own_key, 2), count)]


def centred(rng, extent, width, reach, cuts=(), kind=jnp.bfloat16):
    level = block_levels(rng, extent, cuts, -0.22, 0.18) if cuts else 1.0
    entries = jax.random.normal(rng, extent, jnp.float32) * width * level
    return jnp.minimum(jnp.maximum(entries, -reach), reach).astype(kind)


def bell_draw_with(own_key, dims, width, bound, pieces, heavy, kind=jnp.bfloat16):
    values = width * jax.random.normal(own_key, dims, jnp.float32)
    if pieces:
        values = values * block_levels(own_key, dims, pieces, -0.22, 0.18)
    return jnp.clip(strengthened(values, jax.random.fold_in(own_key, 3), *heavy), -bound, bound).astype(kind)


def setup_inputs(seed: int = 0) -> dict:
    splits = jax.random.split(jax.random.key(seed), 10)
    tokens = centred(splits[0], (TOKENS, D), 1.0, 6.0, ((0, 32),))
    gain = jnp.clip(1.0 + 0.1 * jax.random.normal(splits[1], (D,), jnp.float32), 0.5, 1.5)
    bias = centred(splits[2], (D,), 0.3, 1.5, (), jnp.float32)
    w_qkv = centred(splits[3], (D, 3 * D), D ** -0.5, 0.1875)
    w_out = centred(splits[4], (D, D), (max(D // 64, 16)) ** -0.5, 1.5)
    w_up = centred(splits[5], (D, FF), D ** -0.5, 0.1875, ((1, 4),))
    w_down = centred(splits[6], (FF, D), FF ** -0.5, 0.09375, ((0, 4),))
    lengths = jax.vmap(lambda own: uneven(own, NDOC, ROW, MOST, 2))(jax.random.split(splits[7], ROWS)).reshape((ROWS, NDOC)).astype(jnp.int32)
    grad_out = bell_draw_with(splits[8], (TOKENS, D), 1.0, 6.0, ((0, 32),), (0, 1, 32, 2.75))
    return {"tokens": tokens, "gain": gain, "bias": bias, "w_qkv": w_qkv, "w_out": w_out, "w_up": w_up, "w_down": w_down, "lengths": lengths, "grad_out": grad_out}


@jax.custom_vjp
def low(v):
    return lax.optimization_barrier(v.astype(jnp.bfloat16)).astype(jnp.float32)

@jax.custom_vjp
def low_back(v):
    return v

def low_keep(v):
    return (low(v), None)

def low_pass(kept, grad):
    return (grad,)

def back_keep(v):
    return (v, None)

def back_low(kept, grad):
    return (low(grad),)
low.defvjp(low_keep, low_pass)
low_back.defvjp(back_keep, back_low)
EPSILON = 1e-05
HIGHEST = lax.Precision.HIGHEST

def product(left, right):
    return jnp.dot(left, right, precision=HIGHEST, preferred_element_type=jnp.float32)

def documents(lengths, row_len):
    row_ends = jnp.cumsum(lengths).astype(jnp.int32)
    places = jnp.arange(row_len, dtype=jnp.int32)
    passed = places[:, None] >= row_ends[None, :]
    doc_ids = lax.optimization_barrier(jnp.sum(passed.astype(jnp.int32), axis=1)).astype(jnp.int32)
    starts = lax.optimization_barrier(jnp.sum(jnp.where(passed, lengths[None, :], 0), axis=1)).astype(jnp.int32)
    return (doc_ids, places, places - starts)

def rotary(positions):
    halves = jnp.arange(ROT // 2).astype(jnp.float32)
    rates = jnp.exp(halves * (-2.0 * math.log(10000.0) / ROT))
    angles = positions.astype(jnp.float32)[:, None] * rates[None, :]
    return (jnp.cos(angles), jnp.sin(angles))

def rotate(vectors, cosine_table, sine_table):
    half_rot = ROT // 2
    first_half = vectors[..., :half_rot]
    second_half = vectors[..., half_rot:ROT]
    cosine_part = cosine_table[:, None, :]
    sine_part = sine_table[:, None, :]
    return jnp.concatenate([first_half * cosine_part - second_half * sine_part, second_half * cosine_part + first_half * sine_part, vectors[..., ROT:]], axis=-1)

def gelu_value(inputs):
    return 0.5 * inputs * (1.0 + lax.erf(inputs * 0.7071067811865476))

def row_attention(row_joined, lengths):
    doc_ids, places, positions = documents(lengths, ROW)
    cosine_table, sine_table = rotary(positions)
    queries = low(rotate(row_joined[:, :D].reshape(ROW, H, HD), cosine_table, sine_table))
    keys_rot = low(rotate(row_joined[:, D:2 * D].reshape(ROW, H, HD), cosine_table, sine_table))
    values = low(row_joined[:, 2 * D:].reshape(ROW, H, HD))
    raw_scores = jnp.einsum('qhd,khd->hqk', queries, keys_rot, precision=HIGHEST)
    allowed = (doc_ids[:, None] == doc_ids[None, :]) & (places[None, :] <= places[:, None])
    scores = jnp.where(allowed[None], low_back(raw_scores) * HD ** (-0.5), -1e+30)
    highest = lax.optimization_barrier(jnp.max(scores, axis=-1, keepdims=True))
    exponent = jnp.exp(scores - highest)
    weights = exponent / lax.optimization_barrier(jnp.sum(exponent, axis=-1, keepdims=True))
    mixed_heads = jnp.einsum('hqk,khd->qhd', low(weights), values, precision=HIGHEST)
    return low(low_back(mixed_heads.reshape(ROW, D)))

def attend_one(row_pair):
    return row_attention(row_pair[0], row_pair[1])

def block(tokens, gain, bias, w_qkv, w_out, w_up, w_down, lengths):
    average = lax.optimization_barrier(jnp.mean(tokens, axis=-1, keepdims=True))
    centered = tokens - average
    variance = lax.optimization_barrier(jnp.mean(centered * centered, axis=-1, keepdims=True))
    normed = low(centered * lax.rsqrt(variance + EPSILON) * gain + bias)
    joined = low_back(product(normed, w_qkv))
    heads = lax.map(jax.checkpoint(attend_one), (joined.reshape(ROWS, ROW, 3 * D), lengths))
    attention = product(heads.reshape(TOKENS, D), w_out)
    up_proj = low_back(product(normed, w_up))
    hidden = low(gelu_value(up_proj))
    mixed = product(hidden, w_down)
    return tokens + attention + mixed

def reference(tokens, gain, bias, w_qkv, w_out, w_up, w_down, lengths, grad_out):
    floats = [array_in.astype(jnp.float32) for array_in in (tokens, gain, bias, w_qkv, w_out, w_up, w_down)]

    def forward(tokens_f, gain_f, bias_f, qkv_f, out_f, up_f, down_f):
        return block(tokens_f, gain_f, bias_f, qkv_f, out_f, up_f, down_f, lengths)
    result, pullback = jax.vjp(forward, *floats)
    d_tokens, d_gain, d_bias, d_qkv, d_out, d_up, d_down = pullback(grad_out.astype(jnp.float32))
    return (result.astype(jnp.bfloat16), d_tokens, d_gain, d_bias, d_qkv, d_out, d_up, d_down)
```

```python
import functools
import math

import jax
import jax.numpy as jnp
from jax import lax
from jax.experimental import pallas as pl
from jax.experimental.pallas import tpu as pltpu
from jax.sharding import PartitionSpec as P

D = 1024
HD = 64
ROW = 1024
EPSILON = 1e-05
ROOT_HALF = 0.7071067811865476
NORMAL_PEAK = 0.3989422804014327
BF = jnp.bfloat16
F32 = jnp.float32
QB = 256
HALF = D // 2
MiB = 1 << 20
MESH = pl.DeviceIdType.MESH


def nn(a, b):
    return lax.dot_general(a, b, (((1,), (0,)), ((), ())), preferred_element_type=F32)


def nt(a, b):
    return lax.dot_general(a, b, (((1,), (1,)), ((), ())), preferred_element_type=F32)


def tn(a, b):
    return lax.dot_general(a, b, (((0,), (0,)), ((), ())), preferred_element_type=F32)


def layer_norm(x):
    mean = jnp.mean(x, axis=-1, keepdims=True)
    centered = x - mean
    var = jnp.mean(centered * centered, axis=-1, keepdims=True)
    inverse = lax.rsqrt(var + EPSILON)
    return centered * inverse, inverse


def doc_start(lengths, row, places):
    start = jnp.zeros_like(places)
    end = jnp.zeros((1, 1), jnp.int32)
    for d in range(8):
        end = end + lengths[row, 0:1, d : d + 1]
        start = jnp.where(places >= end, end, start)
    return start


def rotary_tables(lengths, row, rates):
    places = lax.broadcasted_iota(jnp.int32, (8, ROW), 1)
    pos = places - doc_start(lengths, row, places)
    angles = pos.astype(F32) * rates
    cosine, sine = jnp.cos(angles), jnp.sin(angles)
    ones, zeros = jnp.ones((48, ROW), F32), jnp.zeros((8, ROW), F32)
    pad = jnp.zeros((48, ROW), F32)
    table = lambda *parts: jnp.transpose(jnp.concatenate(parts * 2, axis=0))
    return (
        table(cosine, cosine, ones),
        table(-sine, zeros, pad),
        table(zeros, sine, pad),
    )


def rotate(x, cosine, sine_a, sine_b):
    return x * cosine + pltpu.roll(x, 120, 1) * sine_a + pltpu.roll(x, 8, 1) * sine_b


def rotate_back(x, cosine, sine_a, sine_b):
    return x * cosine - pltpu.roll(x, 120, 1) * sine_a - pltpu.roll(x, 8, 1) * sine_b


def band(i):
    return max(0, i - 2) * QB, (i + 1) * QB


MASK_AT = [sum(band(k)[1] - band(k)[0] for k in range(i)) for i in range(5)]


def gelu_and_slope(u):
    bell = 0.5 * (1.0 + lax.erf(u * ROOT_HALF))
    return u * bell, bell + u * jnp.exp(-0.5 * u * u) * NORMAL_PEAK


def aligned(start, unit):
    return pl.multiple_of(start, unit)


def rows(r, size):
    return pl.ds(aligned(r * size, size), size)
class Links:
    def __init__(self, dp, mlp, send_sems, recv_sems):
        self.nb, self.mlp = (dp // 2).bit_length() - 1, mlp
        self.d, self.z = lax.axis_index("dp"), lax.axis_index("mlp")
        self.core = lax.rem(self.d, 2)
        self.bits = [self.bit(self.d, 2 << (self.nb - 1 - i)) for i in range(self.nb)]
        self.send_sems, self.recv_sems, self.count = send_sems, recv_sems, 0

    @staticmethod
    def bit(index, weight):
        return lax.rem(index // weight, 2)

    def flip(self, index, weight):
        return index + weight * (1 - 2 * self.bit(index, weight))

    def sibling(self):
        return (self.flip(self.d, 1), self.z)

    def plane(self, i):
        return (self.flip(self.d, 2 << (self.nb - 1 - i)), self.z)

    def along(self, offset):
        return (self.d, lax.rem(self.z + offset, self.mlp))

    def pairs(self):
        out = [self.sibling()] + [self.plane(i) for i in range(self.nb)]
        return out + [(self.d, self.flip(self.z, 1 << b)) for b in range(self.mlp.bit_length() - 1)]

    def copy(self, src, dst, device):
        k, self.count = self.count, self.count + 1
        return pltpu.make_async_remote_copy(
            src_ref=src,
            dst_ref=dst,
            send_sem=self.send_sems.at[k],
            recv_sem=self.recv_sems.at[k],
            device_id=device,
            device_id_type=MESH,
        )

    def order(self, arr):
        return list(range(self.nb)) if arr == 0 else list(range(self.nb))[::-1]

    def at(self, done, current, value):
        out = [slice(None)] * self.nb
        for i in done:
            out[i] = self.bits[i]
        if current is not None:
            out[current] = value
        return tuple(out)

    def place(self, p):
        return tuple(lax.rem(p // (1 << (self.nb - 1 - i)), 2) for i in range(self.nb))

    def mine(self):
        return tuple(self.bits)


def start_all(copies):
    for copy in copies:
        copy.start()
    return copies


def wait_all(copies):
    for copy in copies:
        copy.wait()


def whole_kernel(
    dp, mlp,
    len_own, rates, gain, bias, tokens, grad_out, w_qkv, w_out, w_up, w_down,
    result, d_tokens, sums_out, d_up, d_down, G, Gs, up_all, down_all, heads_out, gj_out,
    n, nT, g, gT, wup, wdown, ring, recv, zr, fin, zf, swap_out, swap_in, lens, sum_send, sum_recv, up_st, down_st,
    send_sems, recv_sems, sems, stream, free_sem,
):
    L = Links(dp, mlp, send_sems, recv_sems)
    nb, core, z = L.nb, L.core, L.z
    places = 1 << nb
    R = D // places

    barrier = pltpu.get_barrier_semaphore()
    greeted = [L.sibling()] + [L.plane(i) for i in range(nb)] + [L.along(o) for o in range(1, mlp)]
    for device in greeted:
        pl.semaphore_signal(barrier, inc=1, device_id=device, device_id_type=MESH)
    pl.semaphore_wait(barrier, len(greeted))

    used = [0]

    def make(src, dst):
        k, used[0] = used[0], used[0] + 1
        return pltpu.make_async_copy(src, dst, sems.at[k])

    def local(src, dst):
        copy = make(src, dst)
        copy.start()
        return copy

    own, sib = pl.ds(0, ROW), pl.ds(ROW, ROW)
    half_cols = pl.ds(aligned(core * HALF, HALF), HALF)
    every = (slice(None),) * nb

    len_swap = L.copy(len_own, lens.at[1], L.sibling())
    tok_swap = L.copy(tokens, n.at[sib], L.sibling())
    g_swap = L.copy(grad_out, g.at[sib], L.sibling())
    start_all([len_swap, tok_swap])
    tok_load = local(tokens, n.at[own])
    len_load = local(len_own, lens.at[0])
    g_swap.start()
    g_load = local(grad_out, g.at[own])
    w_loads = []
    for part in range(3):
        cols = pl.ds(aligned(part * D + core * HALF, HALF), HALF)
        w_loads.append(local(w_qkv.at[every + (slice(None), cols)], wup.at[part]))
    w_loads.append(local(w_out.at[core], wdown.at[0]))

    my = L.mine()
    gather_z = []
    for o in range(1, mlp):
        gather_z.append(L.copy(w_up.at[my + (slice(None), half_cols)], up_all.at[(z,) + my], L.along(o)))
        gather_z.append(L.copy(w_down.at[(core,) + my], down_all.at[(z,) + my], L.along(o)))
    start_all(gather_z)

    def gather_plane(j):
        out = []
        for arr, ref in enumerate((up_all, down_all)):
            order = L.order(arr)
            idx = L.at(order[: j + 1], None, None)
            for o in range(1, mlp):
                view = ref.at[(lax.rem(z + o, mlp),) + idx]
                out.append(L.copy(view, view, L.plane(order[j])))
        return out

    gather_p = [gather_plane(j) for j in range(nb)][::-1]

    UNITS = 2 + mlp
    SLOTS = ring.shape[0]

    def plane_stage(u, j):
        slot, out = u % SLOTS, []
        for arr in range(2):
            order = L.order(arr)
            here = order[j]
            src = ring.at[(slot, arr) + L.at(order[:j], here, 1 - L.bits[here])]
            out.append(L.copy(src, recv[j].at[u % 2, arr], L.plane(here)))
        return out

    stage = {(u, j): plane_stage(u, j) for u in range(UNITS) for j in range(nb)}

    def lead_indices(depth):
        out = [()]
        for _ in range(depth):
            out = [t + (b,) for t in out for b in range(2)]
        return out

    def plane_add(u, j):
        slot = u % SLOTS
        wait_all(stage[u, j])
        step = min(R, 64)
        for arr in range(2):
            order = L.order(arr)
            done = order[: j + 1]
            rest = sorted(order[j + 1 :])
            for lead in lead_indices(len(rest)):
                idx = [None] * nb
                for i in done:
                    idx[i] = L.bits[i]
                for i, b in zip(rest, lead):
                    idx[i] = b
                target = ring.at[(slot, arr) + tuple(idx)]
                source = recv[j].at[(u % 2, arr) + lead]

                @pl.loop(0, R // step)
                def _(r):
                    total = target[rows(r, step)].astype(F32) + source[rows(r, step)].astype(F32)
                    target[rows(r, step)] = total.astype(BF)

    ZC = HALF // mlp
    cols_of = lambda w: pl.ds(aligned(w * ZC, ZC), ZC)

    def z_scatter(u):
        out = []
        for arr in range(2):
            for o in range(1, mlp):
                there = lax.rem(z + o, mlp)
                src = ring.at[(u % SLOTS, arr) + my + (slice(None), cols_of(there))]
                out.append(L.copy(src, zr.at[u, o - 1, arr], L.along(o)))
        return out

    def z_gather(u):
        out = []
        for arr in range(2):
            view = G.at[(u, arr) + my + (slice(None), cols_of(z))]
            for o in range(1, mlp):
                out.append(L.copy(fin.at[u, arr], view, L.along(o)))
        return out

    def g_plane(u, j):
        out = []
        for arr in range(2):
            order = L.order(arr)
            view = G.at[(u, arr) + L.at(order[: j + 1], None, None)]
            out.append(L.copy(view, view, L.plane(order[j])))
        return out

    scatter_z = [z_scatter(u) for u in range(2)]
    back_z = [z_gather(u) for u in range(2)]
    back_p = [[g_plane(u, j) for j in range(nb)][::-1] for u in range(2)]
    back_c = [L.copy(G.at[u], Gs.at[u], L.sibling()) for u in range(2)]
    kept = [[make(fin.at[u, arr], G.at[(u, arr) + my + (slice(None), cols_of(z))]) for arr in range(2)] for u in range(2)]

    def z_sum(u):
        wait_all(scatter_z[u])
        for arr in range(2):
            total = ring[(u % SLOTS, arr) + my + (slice(None), cols_of(z))].astype(F32)
            for o in range(mlp - 1):
                total = total + zr[u, o, arr].astype(F32)
            fin[u, arr] = total.astype(BF)
        start_all(back_z[u])
        start_all(kept[u])

    def z_back(u):
        wait_all(back_z[u])
        wait_all(kept[u])

    len_load.wait()
    tok_load.wait()

    @pl.loop(0, ROW // QB)
    def _(r):
        xhat, _ = layer_norm(n[rows(r, QB)].astype(F32))
        normed = (xhat * gain[...] + bias[...]).astype(BF)
        n[rows(r, QB)] = normed
        nT[:, rows(r, QB)] = jnp.transpose(normed)

    tok_swap.wait()

    @pl.loop(ROW // QB, 2 * ROW // QB)
    def _(r):
        xhat, _ = layer_norm(n[rows(r, QB)].astype(F32))
        normed = (xhat * gain[...] + bias[...]).astype(BF)
        n[rows(r, QB)] = normed
        nT[:, rows(r, QB)] = jnp.transpose(normed)

    g_load.wait()
    g_swap.wait()

    @pl.loop(0, 2 * ROW // QB)
    def _(r):
        gT[:, rows(r, QB)] = jnp.transpose(g[rows(r, QB)])

    len_swap.wait()
    wait_all(w_loads)
    lane_low = lax.broadcasted_iota(jnp.int32, (1, 128), 1) < HD

    def attention(tables, mask, qs, ks, vs, ghs, gkT, gvT, heads, gj):
        for row in range(2):
            for k, t in enumerate(rotary_tables(lens, row, rates[...])):
                tables[row, k] = t
            for i in range(ROW // QB):
                lo, hi = band(i)
                query = lax.broadcasted_iota(jnp.int32, (QB, 128), 0) + i * QB
                start = doc_start(lens, row, query)
                for j in range(lo, hi, 128):
                    key = lax.broadcasted_iota(jnp.int32, (QB, 128), 1) + j
                    allowed = (key >= start) & (key <= query)
                    at = MASK_AT[i] + j - lo
                    mask[row, :, at : at + 128] = jnp.where(allowed, 0.0, -1e30)

        def attend(row, pair, col):
            out_cols = pl.ds(col, 128)
            gkT[...] = jnp.zeros_like(gkT)
            gvT[...] = jnp.zeros_like(gvT)
            for i in range(ROW // QB):
                lo, hi = band(i)
                width = hi - lo
                qb = qs[pair, i * QB : (i + 1) * QB]
                gb = ghs[pair, i * QB : (i + 1) * QB]
                kb, vb = ks[pair, lo:hi], vs[pair, lo:hi]
                hidden = mask[row, :, MASK_AT[i] : MASK_AT[i] + width]
                heads_pair, gq_pair = [], []
                for h in range(2):
                    mine = lane_low if h == 0 else ~lane_low
                    qm = jnp.where(mine, qb, jnp.zeros_like(qb))
                    gm = jnp.where(mine, gb, jnp.zeros_like(gb))
                    scores = nt(qm, kb) + hidden
                    exponent = jnp.exp(scores - jnp.max(scores, axis=-1, keepdims=True))
                    mixed = nn(exponent.astype(BF), jnp.where(mine, vb, jnp.ones_like(vb)))
                    total = jnp.where(mine, pltpu.roll(mixed, 64, 1), mixed)
                    inverse = 1.0 / total
                    head = mixed * inverse
                    weights = exponent * jnp.concatenate([inverse] * (width // 128), axis=1)
                    grad_w = nt(gm, vb)
                    centre = jnp.sum(gm.astype(F32) * head, axis=-1, keepdims=True)
                    grad_raw = (weights * (grad_w - centre)).astype(BF)
                    gq_pair.append(nn(grad_raw, kb))
                    gkT[:, lo:hi] += tn(qm, grad_raw)
                    gvT[:, lo:hi] += tn(gm, weights.astype(BF))
                    heads_pair.append(head)
                here = pl.ds(aligned(row * ROW + i * QB, QB), QB)
                heads[here, out_cols] = jnp.where(lane_low, *heads_pair).astype(BF)
                gq = jnp.where(lane_low, *gq_pair) * (HD**-0.5)
                t = [tables[row, k, i * QB : (i + 1) * QB] for k in range(3)]
                gj[here, out_cols] = rotate_back(gq, *t).astype(BF)
            for i in range(ROW // QB):
                here = pl.ds(aligned(row * ROW + i * QB, QB), QB)
                t = [tables[row, k, i * QB : (i + 1) * QB] for k in range(3)]
                gk = jnp.transpose(gkT[:, i * QB : (i + 1) * QB])
                gj[here, pl.ds(aligned(HALF + col, 128), 128)] = rotate_back(gk, *t).astype(BF)
                gv = jnp.transpose(gvT[:, i * QB : (i + 1) * QB])
                gj[here, pl.ds(aligned(2 * HALF + col, 128), 128)] = gv.astype(BF)

        PB = 512

        def project(group, row):
            gcol = aligned(group * 256, 256)

            @pl.loop(0, ROW // PB)
            def _(r):
                here = pl.ds(aligned(row * ROW + r * PB, PB), PB)
                inside = rows(r, PB)
                nb_, gb = n[here], g[here]
                t = [tables[row, k, inside] for k in range(3)]
                block = lambda part: wup[(part,) + every + (slice(None), pl.ds(gcol, 256))].reshape(D, 256)
                q, k, v = [nn(nb_, block(part)) for part in range(3)]
                gh = nt(gb, wout_rows(group))
                for p in range(2):
                    cut = slice(p * 128, p * 128 + 128)
                    qs[p, inside] = rotate(q[:, cut], *t).astype(BF) * jnp.asarray(HD**-0.5, BF)
                    ks[p, inside] = rotate(k[:, cut], *t).astype(BF)
                    vs[p, inside] = v[:, cut].astype(BF)
                    ghs[p, inside] = gh[:, cut].astype(BF)

        def wout_rows(group):
            return wdown[(0, group)].reshape(256, D)

        def group_grads(u):
            gcol = u * 256

            @pl.loop(0, places)
            def _(p):
                here = rows(p, R)
                idx = L.place(p)
                for part in range(3):
                    arr, at = part // 2, (part % 2) * 256
                    lo = part * HALF + gcol
                    ring[(u, arr) + idx + (slice(None), pl.ds(at, 256))] = nn(nT[here], gj[:, lo : lo + 256]).astype(BF)
                ring[(u, 1) + idx + (slice(None), pl.ds(256, 256))] = nn(gT[here], heads[:, gcol : gcol + 256]).astype(BF)

        def after(step):
            if step == 3:
                group_grads(0)
                start_all(stage[0, 0])
                wait_all(gather_z)
                start_all(gather_p[0])
            if 4 <= step <= 6:
                done = step - 4
                lo, hi = done * nb // 3, (done + 1) * nb // 3
                if step == 6:
                    hi = nb
                for j in range(lo, hi):
                    plane_add(0, j)
                    if j + 1 < nb:
                        start_all(stage[0, j + 1])
                    else:
                        start_all(scatter_z[0])
            if step == 5:
                for j in range(nb - 1):
                    wait_all(gather_p[j])
                    start_all(gather_p[j + 1])
            if step == 7:
                group_grads(1)
                z_sum(0)
                start_all(stage[1, 0])

        @pl.loop(0, 8)
        def _(step):
            group, row, pair = step // 4, lax.rem(step // 2, 2), lax.rem(step, 2)

            @pl.when(pair == 0)
            def _():
                project(group, row)

            attend(row, pair, aligned(step // 4 * 256 + pair * 128, 128))

            for t in range(3, 8):

                @pl.when(step == t)
                def _():
                    after(t)

        wait_all([local(heads, heads_out), local(gj, gj_out)])

    V = pltpu.VMEM
    pl.run_scoped(
        attention,
        V((2, 3, ROW, 128), F32),
        V((2, QB, MASK_AT[4]), F32),
        *[V((2, ROW, 128), BF)] * 4,
        *[V((128, ROW), F32)] * 2,
        V((2 * ROW, HALF), BF),
        V((2 * ROW, 3 * HALF), BF),
    )

    def feed_forward(acc_r, acc_g, gjb, hdb, hid, gup):
        blocks = 2 * ROW // QB

        def stream_in(r, slot):
            return (
                pltpu.make_async_copy(heads_out.at[rows(r, QB)], hdb.at[slot], stream.at[0, slot]),
                pltpu.make_async_copy(gj_out.at[rows(r, QB)], gjb.at[slot], stream.at[1, slot]),
            )

        up_slot = lambda k: (3, 0, 1, 2)[k % 4]
        down_slot = lambda k: (k + 1) % 2

        def weights_in(k):
            if k == mlp - 1:
                return [
                    local(w_up.at[every + (slice(None), half_cols)], wup.at[up_slot(k)]),
                    local(w_down.at[core], wdown.at[down_slot(k)]),
                ]
            s = lax.rem(z + 1 + k, mlp)
            return [local(up_all.at[s], wup.at[up_slot(k)]), local(down_all.at[s], wdown.at[down_slot(k)])]

        start_all(stream_in(0, 0))

        @pl.loop(0, blocks)
        def _(r):
            slot = lax.rem(r, 2)

            @pl.when(r + 1 < blocks)
            def _():
                start_all(stream_in(r + 1, 1 - slot))

            wait_all(stream_in(r, slot))
            acc_r[rows(r, QB)] = nn(hdb[slot], wdown[0].reshape(HALF, D))
            total = nt(gjb[slot, :, :HALF], wup[0].reshape(D, HALF))
            for part in range(1, 3):
                total += nt(gjb[slot, :, part * HALF : (part + 1) * HALF], wup[part].reshape(D, HALF))
            acc_g[rows(r, QB)] = total

        z_back(0)
        start_all(back_p[0][0])
        wait_all(gather_p[nb - 1])
        plane_add(1, 0)
        if nb > 1:
            start_all(stage[1, 1])
        pending = weights_in(0)

        z_send = {}

        def after_tokens(k):
            if k == 0:
                for j in range(1, nb):
                    plane_add(1, j)
                    if j + 1 < nb:
                        start_all(stage[1, j + 1])
                start_all(scatter_z[1])
                for j in range(nb - 1):
                    wait_all(back_p[0][j])
                    start_all(back_p[0][j + 1])
            else:
                u = k + 1
                plane_add(u, 0)
                if nb > 1:
                    start_all(stage[u, 1])
            if k == 1:
                z_sum(1)
                wait_all(back_p[0][nb - 1])
                back_c[0].start()
            if k == 2:
                for j in range(nb - 1):
                    wait_all(back_p[1][j])
                    start_all(back_p[1][j + 1])
            if k == mlp - 1:
                wait_all(back_p[1][nb - 1])
                back_c[1].start()

        def send_z(u):
            for j in range(1, nb):
                plane_add(u, j)
                if j + 1 < nb:
                    start_all(stage[u, j + 1])
            k = u - 2
            z_send[k] = [
                L.copy(ring.at[(u % SLOTS, arr) + my], zf.at[k, arr], L.along(1 + k)) for arr in range(2)
            ]
            start_all(z_send[k])

        def after_grads(k):
            u = k + 2
            if k >= 1:
                send_z(u - 1)
            if k == 1:
                z_back(1)
                start_all(back_p[1][0])
            start_all(stage[u, 0])

        swap_r = L.copy(nT.at[:, pl.ds(0, D)], n.at[sib], L.sibling())
        swap_g = L.copy(nT.at[:, pl.ds(D, D)], g.at[sib], L.sibling())

        for k in range(mlp):
            last = k == mlp - 1
            wait_all(pending)
            if not last:
                pending = weights_in(k + 1)
            us, ds = up_slot(k), down_slot(k)

            @pl.loop(0, blocks)
            def _(r):
                here = rows(r, QB)
                w1, w2 = wup[us].reshape(D, HALF), wdown[ds].reshape(HALF, D)
                up = nn(n[here], w1)
                hidden, slope = gelu_and_slope(up)
                hidden = hidden.astype(BF)
                hid[here] = hidden
                acc_r[here] += nn(hidden, w2)
                grad = (nt(g[here], w2) * slope).astype(BF)
                gup[here] = grad
                acc_g[here] += nt(grad, w1)

            if last:
                pl.semaphore_signal(free_sem, inc=1, device_id=L.sibling(), device_id_type=MESH)
                tok_again = local(tokens, n.at[own])
            after_tokens(k)
            slot = (k + 2) % SLOTS
            if k + 2 >= SLOTS and k + 2 - SLOTS >= 2:
                wait_all(z_send[k - SLOTS])

            @pl.loop(0, places)
            def _(p):
                ring[(slot, 0) + L.place(p)] = nn(nT[rows(p, R)], gup[...]).astype(BF)

            if last:

                @pl.loop(0, ROW // QB)
                def _(r):
                    there = pl.ds(aligned(ROW + r * QB, QB), QB)
                    nT[rows(r, QB), pl.ds(0, D)] = acc_r[there].astype(BF)
                    nT[rows(r, QB), pl.ds(D, D)] = acc_g[there].astype(BF)

                pl.semaphore_wait(free_sem, 1)
                start_all([swap_r, swap_g])

            @pl.loop(0, places)
            def _(p):
                ring[(slot, 1) + L.place(p)] = nn(gT[rows(p, R)], hid[...]).astype(BF)

            after_grads(k)

        tok_again.wait()
        swap_r.wait()
        swap_g.wait()
        sum_send[0] = jnp.zeros_like(sum_send[0])
        FB = 128

        @pl.loop(0, ROW // FB)
        def _(r):
            here = rows(r, FB)
            there = pl.ds(aligned(ROW + r * FB, FB), FB)
            x = n[here].astype(F32)
            xhat, inverse = layer_norm(x)
            n[here] = (x + acc_r[here] + n[there].astype(F32)).astype(BF)
            grad = acc_g[here] + g[there].astype(F32)
            sum_send[0, 0:1] += jnp.sum(grad * xhat, axis=0, keepdims=True)
            sum_send[0, 1:2] += jnp.sum(grad, axis=0, keepdims=True)
            scaled = grad * gain[...]
            acc_g[here] = g[here].astype(F32) + inverse * (
                scaled
                - jnp.mean(scaled, axis=-1, keepdims=True)
                - xhat * jnp.mean(scaled * xhat, axis=-1, keepdims=True)
            )

        outs = [local(n.at[own], result), local(acc_g.at[pl.ds(0, ROW)], d_tokens)]

        partners = L.pairs()
        adds = [L.copy(sum_send.at[i], sum_recv.at[i], device) for i, device in enumerate(partners)]

        def sum_step(i):
            adds[i].wait()
            sum_send[i + 1] = sum_send[i] + sum_recv[i]
            if i + 1 < len(adds):
                adds[i + 1].start()

        adds[0].start()
        sum_step(0)
        u = mlp + 1
        for j in range(nb):
            plane_add(u, j)
            if j + 1 < nb:
                start_all(stage[u, j + 1])
            if j + 1 < len(adds):
                sum_step(j + 1)
        k = mlp - 1
        for i in range(mlp - 1):
            if i + SLOTS > mlp - 1:
                wait_all(z_send[i])
        slot = u % SLOTS
        S = R // 2
        for arr in range(2):
            for keep in range(2):
                lo = pl.ds(aligned((core if keep else 1 - core) * S, S), S)
                total = ring[(slot, arr) + my + (lo,)].astype(F32)
                for i in range(mlp - 1):
                    total = total + zf[i, arr, lo].astype(F32)
                if keep:
                    (up_st if arr == 0 else down_st)[0] = total
                else:
                    swap_out[arr] = total.astype(BF)
        last_swap = L.copy(swap_out, swap_in, L.sibling())
        last_swap.start()
        for i in range(nb + 1, len(adds)):
            sum_step(i)
        sums_out[...] = sum_send[len(adds)]
        back_c[0].wait()
        back_c[1].wait()
        last_swap.wait()
        up_st[1] = swap_in[0].astype(F32)
        down_st[1] = swap_in[1].astype(F32)
        for i in range(2):
            which = core if i == 0 else 1 - core
            outs.append(local(up_st.at[i], d_up.at[:, pl.ds(aligned(which * HALF, HALF), HALF)]))
            outs.append(local(down_st.at[i], d_down.at[:, pl.ds(aligned(which * HALF, HALF), HALF)]))
        wait_all(outs)

    pl.run_scoped(
        feed_forward,
        V((2 * ROW, D), F32),
        V((2 * ROW, D), F32),
        V((2, QB, 3 * HALF), BF),
        V((2, QB, HALF), BF),
        V((2 * ROW, HALF), BF),
        V((2 * ROW, HALF), BF),
    )


def convert_kernel(mine, theirs, d_qkv, d_out):
    core = lax.rem(lax.axis_index("dp"), 2)
    for who, ref in ((core, mine), (1 - core, theirs)):
        for u in range(2):
            lane = who * HALF + u * 256
            for part in range(3):
                at = (part % 2) * 256
                d_qkv[:, pl.ds(aligned(part * D + lane, 256), 256)] = ref[u, part // 2, :, at : at + 256].astype(F32)
            d_out[pl.ds(aligned(lane, 256), 256)] = jnp.transpose(ref[u, 1, :, 256:].astype(F32))


def convert(mine, theirs):
    block = pl.BlockSpec((2, 2, QB, HALF), lambda r: (0, 0, r, 0))
    return pl.pallas_call(
        convert_kernel,
        grid=(D // QB,),
        out_shape=[jax.ShapeDtypeStruct((D, 3 * D), F32), jax.ShapeDtypeStruct((D, D), F32)],
        in_specs=[block, block],
        out_specs=[pl.BlockSpec((QB, 3 * D), lambda r: (r, 0)), pl.BlockSpec((D, QB), lambda r: (0, r))],
        cost_estimate=pl.CostEstimate(flops=10**7, bytes_accessed=24 * MiB, transcendentals=0),
        compiler_params=pltpu.CompilerParams(vmem_limit_bytes=48 * MiB),
        name="convert",
    )(mine, theirs)


def shards(dp, mlp, tokens, gain, bias, w_qkv, w_out, w_up, w_down, lengths, grad_out):
    nb = (dp // 2).bit_length() - 1
    places = 1 << nb
    bits, R, Rd = (2,) * nb, D // places, HALF // places
    slots = 3
    rates = jnp.exp(jnp.arange(8).astype(F32) * (-2.0 * math.log(10000.0) / 16)).reshape(8, 1)
    anyspec, vm = pl.BlockSpec(memory_space=pl.ANY), pl.BlockSpec(memory_space=pltpu.VMEM)
    S = jax.ShapeDtypeStruct
    V = pltpu.VMEM
    two = 2 * ROW
    steps = nb + mlp.bit_length()
    gathered = (2, 2) + bits + (R, HALF)
    out_shape = [
        S((ROW, D), BF), S((ROW, D), F32), S((8, D), F32), S((R // 2, D), F32), S((R // 2, D), F32),
        S(gathered, BF), S(gathered, BF), S((mlp,) + bits + (R, HALF), BF), S((mlp,) + bits + (Rd, D), BF),
        S((two, HALF), BF), S((two, 3 * HALF), BF),
    ]
    out_specs = [anyspec] * 11
    out_specs[2] = vm
    outs = pl.pallas_call(
        functools.partial(whole_kernel, dp, mlp),
        out_shape=out_shape,
        in_specs=[anyspec, vm, vm, vm] + [anyspec] * 6,
        out_specs=out_specs,
        scratch_shapes=[
            V((two, D), BF), V((D, two), BF), V((two, D), BF), V((D, two), BF),
            V((4,) + bits + (R, HALF), BF), V((2,) + bits + (Rd, D), BF),
            V((slots, 2) + bits + (R, HALF), BF),
            [V((2, 2) + (2,) * (nb - 1 - j) + (R, HALF), BF) for j in range(nb)],
            V((2, mlp - 1, 2, R, HALF // mlp), BF), V((2, 2, R, HALF // mlp), BF), V((mlp - 1, 2, R, HALF), BF),
            V((2, R // 2, HALF), BF), V((2, R // 2, HALF), BF),
            V((2, 8, 128), jnp.int32), V((steps + 1, 8, D), F32), V((steps, 8, D), F32),
            V((2, R // 2, HALF), F32), V((2, R // 2, HALF), F32),
            pltpu.SemaphoreType.DMA((192,)), pltpu.SemaphoreType.DMA((192,)), pltpu.SemaphoreType.DMA((64,)),
            pltpu.SemaphoreType.DMA((2, 2)), pltpu.SemaphoreType.REGULAR,
        ],
        compiler_params=pltpu.CompilerParams(vmem_limit_bytes=63 * MiB, collective_id=0, has_side_effects=True),
        cost_estimate=pl.CostEstimate(flops=120 * 10**9, bytes_accessed=60 * MiB, transcendentals=0),
        name="block",
    )(
        jnp.pad(lengths, ((0, 7), (0, 120))), rates, gain.reshape(1, D), bias.reshape(1, D), tokens, grad_out,
        w_qkv.reshape(bits + (R, 3 * D)), w_out.reshape((2,) + bits + (Rd, D)),
        w_up.reshape(bits + (R, D)), w_down.reshape((2,) + bits + (Rd, D)),
    )
    result, d_tokens, sums, d_up, d_down, mine, theirs = outs[:7]
    d_qkv, d_out = convert(mine.reshape(2, 2, D, HALF), theirs.reshape(2, 2, D, HALF))
    return (result, d_tokens, sums[0], sums[1], d_qkv, d_out, d_up, d_down.T)


def solution(mesh):
    dp, mlp = mesh.shape["dp"], mesh.shape["mlp"]
    rows_in = P(("dp", "mlp"), None)
    in_specs = (rows_in, P(), P(), P(), P(), P(None, "mlp"), P("mlp", None), rows_in, rows_in)
    out_specs = (rows_in, rows_in, P(), P(), P(), P(), P("dp", "mlp"), P("mlp", "dp"))
    body = functools.partial(shards, dp, mlp)
    return jax.shard_map(body, mesh=mesh, in_specs=in_specs, out_specs=out_specs, check_vma=False)
```

```python
import functools
import math

import jax
import jax.numpy as jnp
from jax import lax
from jax.experimental import pallas as pl
from jax.experimental.pallas import tpu as pltpu
from jax.sharding import PartitionSpec as P

D = 1024
HD = 64
ROW = 1024
EPSILON = 1e-05
ROOT_HALF = 0.7071067811865476
NORMAL_PEAK = 0.3989422804014327
BF = jnp.bfloat16
F32 = jnp.float32
QB = 256
HALF = D // 2
MiB = 1 << 20
MESH = pl.DeviceIdType.MESH


def nn(a, b):
    return lax.dot_general(a, b, (((1,), (0,)), ((), ())), preferred_element_type=F32)


def nt(a, b):
    return lax.dot_general(a, b, (((1,), (1,)), ((), ())), preferred_element_type=F32)


def tn(a, b):
    return lax.dot_general(a, b, (((0,), (0,)), ((), ())), preferred_element_type=F32)


def layer_norm(x):
    mean = jnp.mean(x, axis=-1, keepdims=True)
    centered = x - mean
    var = jnp.mean(centered * centered, axis=-1, keepdims=True)
    inverse = lax.rsqrt(var + EPSILON)
    return centered * inverse, inverse


def doc_start(lengths, row, places):
    start = jnp.zeros_like(places)
    end = jnp.zeros((1, 1), jnp.int32)
    for d in range(8):
        end = end + lengths[row, 0:1, d : d + 1]
        start = jnp.where(places >= end, end, start)
    return start


def rotary_tables(lengths, row, rates):
    places = lax.broadcasted_iota(jnp.int32, (8, ROW), 1)
    pos = places - doc_start(lengths, row, places)
    angles = pos.astype(F32) * rates
    cosine, sine = jnp.cos(angles), jnp.sin(angles)
    ones, zeros = jnp.ones((48, ROW), F32), jnp.zeros((8, ROW), F32)
    pad = jnp.zeros((48, ROW), F32)
    table = lambda *parts: jnp.transpose(jnp.concatenate(parts * 2, axis=0))
    return (
        table(cosine, cosine, ones),
        table(-sine, zeros, pad),
        table(zeros, sine, pad),
    )


def rotate(x, cosine, sine_a, sine_b):
    return x * cosine + pltpu.roll(x, 120, 1) * sine_a + pltpu.roll(x, 8, 1) * sine_b


def rotate_back(x, cosine, sine_a, sine_b):
    return x * cosine - pltpu.roll(x, 120, 1) * sine_a - pltpu.roll(x, 8, 1) * sine_b


def band(i):
    return max(0, i - 2) * QB, (i + 1) * QB


MASK_AT = [sum(band(k)[1] - band(k)[0] for k in range(i)) for i in range(5)]


ERFC_RATE = 0.55 * ROOT_HALF
ERFC_TERMS = (
    0.30159098847742044, 0.3907933818624623, -0.04130162875264046,
    0.7595567015262069, -0.5179392414738552, 0.10729981475108823,
)


def gelu_and_slope(u):
    density = jnp.exp(-0.5 * u * u)
    t = pltpu.reciprocal(1.0 + ERFC_RATE * jnp.abs(u))
    poly = 0.5 * ERFC_TERMS[5]
    for term in ERFC_TERMS[4::-1]:
        poly = poly * t + 0.5 * term
    tail = poly * t * density
    bell = jnp.where(u < 0.0, tail, 1.0 - tail)
    return u * bell, bell + u * density * NORMAL_PEAK


def aligned(start, unit):
    return pl.multiple_of(start, unit)


def rows(r, size):
    return pl.ds(aligned(r * size, size), size)
STEP_PLAN = (
    (("W1", 1), ("W2", 0)),
    (("W1", 2),),
    (("W2", 1), ("W3", 0)),
    (("U0", 0), ("W1", 3)),
    (("U0", 1), ("W2", 2)),
    (("U0", 2), ("W3", 1)),
    (("U0", 3), ("W2", 3), ("W3", 2)),
    (("U1", 0), ("U0", 4)),
)
SLICE_PLAN = {
    (0, "init"): (("U0", 5), ("W3", 3)),
    (0, "mid"): (("U1", 1),),
    (0, "tokens"): (("U1", 2), ("U0", 6)),
    (1, "mid"): (("U1", 3),),
    (1, "tokens"): (("F0", 1), ("U1", 4)),
    (1, "down"): (("F0", 2), ("U1", 5)),
    (2, "mid"): (("U1", 6),),
    (2, "tokens"): (("F1", 1),),
    (2, "down"): (("F1", 2),),
    (3, "tokens"): (("F2", 1),),
    (3, "up"): (("F2", 2),),
}


class Links:
    def __init__(self, dp, mlp, send_sems, recv_sems):
        self.nb, self.mlp = (dp // 2).bit_length() - 1, mlp
        self.d, self.z = lax.axis_index("dp"), lax.axis_index("mlp")
        self.core = lax.rem(self.d, 2)
        self.bits = [self.bit(self.d, 2 << (self.nb - 1 - i)) for i in range(self.nb)]
        self.send_sems, self.recv_sems, self.count = send_sems, recv_sems, 0

    @staticmethod
    def bit(index, weight):
        return lax.rem(index // weight, 2)

    def flip(self, index, weight):
        return index + weight * (1 - 2 * self.bit(index, weight))

    def sibling(self):
        return (self.flip(self.d, 1), self.z)

    def plane(self, i):
        return (self.flip(self.d, 2 << (self.nb - 1 - i)), self.z)

    def along(self, offset):
        return (self.d, lax.rem(self.z + offset, self.mlp))

    def pairs(self):
        out = [self.sibling()] + [self.plane(i) for i in range(self.nb)]
        return out + [(self.d, self.flip(self.z, 1 << b)) for b in range(self.mlp.bit_length() - 1)]

    def copy(self, src, dst, device):
        k, self.count = self.count, self.count + 1
        return pltpu.make_async_remote_copy(
            src_ref=src,
            dst_ref=dst,
            send_sem=self.send_sems.at[k],
            recv_sem=self.recv_sems.at[k],
            device_id=device,
            device_id_type=MESH,
        )

    def order(self, arr):
        return list(range(self.nb)) if arr == 0 else list(range(self.nb))[::-1]

    def at(self, done, current, value):
        out = [slice(None)] * self.nb
        for i in done:
            out[i] = self.bits[i]
        if current is not None:
            out[current] = value
        return tuple(out)

    def place(self, p):
        return tuple(lax.rem(p // (1 << (self.nb - 1 - i)), 2) for i in range(self.nb))

    def mine(self):
        return tuple(self.bits)


def start_all(copies):
    for copy in copies:
        copy.start()
    return copies


def wait_all(copies):
    for copy in copies:
        copy.wait()


class Chain:
    def __init__(self, begin, end, marks):
        self.begin, self.end, self.marks, self.at = begin, end, marks, -1

    def to(self, mark):
        goal = self.marks[mark]
        while self.at < goal:
            if self.at >= 0:
                self.end[self.at]()
            self.at += 1
            if self.at < len(self.begin):
                self.begin[self.at]()


def whole_kernel(
    dp, mlp,
    len_own, rates, gain, bias, tokens, grad_out, w_qkv, w_out, w_up, w_down,
    result, d_tokens, sums_out, d_up, d_down, G, Gs, up_all, down_all,
    n, nT, g, gT, wup, wdown, ring, recv, zr, fin, zf, swap_out, swap_in, lens, sum_send, sum_recv, up_st, down_st,
    hid, gj,
    send_sems, recv_sems, sems, free_sem,
):
    L = Links(dp, mlp, send_sems, recv_sems)
    nb, core, z = L.nb, L.core, L.z
    places = 1 << nb
    R = D // places

    barrier = pltpu.get_barrier_semaphore()
    greeted = [L.sibling()] + [L.plane(i) for i in range(nb)] + [L.along(o) for o in range(1, mlp)]
    for device in greeted:
        pl.semaphore_signal(barrier, inc=1, device_id=device, device_id_type=MESH)
    pl.semaphore_wait(barrier, len(greeted))

    used = [0]

    def make(src, dst):
        k, used[0] = used[0], used[0] + 1
        return pltpu.make_async_copy(src, dst, sems.at[k])

    def local(src, dst):
        copy = make(src, dst)
        copy.start()
        return copy

    own, sib = pl.ds(0, ROW), pl.ds(ROW, ROW)
    half_cols = pl.ds(aligned(core * HALF, HALF), HALF)
    every = (slice(None),) * nb

    len_swap = L.copy(len_own, lens.at[1], L.sibling())
    tok_swap = L.copy(tokens, n.at[sib], L.sibling())
    g_swap = L.copy(grad_out, g.at[sib], L.sibling())
    start_all([len_swap, tok_swap])
    tok_load = local(tokens, n.at[own])
    len_load = local(len_own, lens.at[0])
    g_swap.start()
    g_load = local(grad_out, g.at[own])
    w_loads = []
    for part in range(3):
        cols = pl.ds(aligned(part * D + core * HALF, HALF), HALF)
        w_loads.append(local(w_qkv.at[every + (slice(None), cols)], wup.at[part]))
    w_loads.append(local(w_out.at[core], wdown.at[0]))

    my = L.mine()

    def gather(o):
        there = lax.rem(z + o, mlp)
        stages = [
            [
                L.copy(w_up.at[my + (slice(None), half_cols)], up_all.at[(z,) + my], L.along(mlp - o)),
                L.copy(w_down.at[(core,) + my], down_all.at[(z,) + my], L.along(mlp - o)),
            ]
        ]
        for j in reversed(range(nb)):
            copies = []
            for arr, ref in enumerate((up_all, down_all)):
                order = L.order(arr)
                view = ref.at[(there,) + L.at(order[: j + 1], None, None)]
                copies.append(L.copy(view, view, L.plane(order[j])))
            stages.append(copies)
        marks = {0: 0, 1: 1, 2: 1 + nb // 2, 3: 1 + nb}
        return Chain(
            [functools.partial(start_all, s) for s in stages],
            [functools.partial(wait_all, s) for s in stages],
            marks,
        )

    slice_chain = [None] + [gather(o) for o in range(1, mlp)]

    UNITS = 2 + mlp
    SLOTS = ring.shape[0]

    def plane_stage(u, j):
        slot, out = u % SLOTS, []
        for arr in range(2):
            order = L.order(arr)
            here = order[j]
            src = ring.at[(slot, arr) + L.at(order[:j], here, 1 - L.bits[here])]
            out.append(L.copy(src, recv[j].at[u % 2, arr], L.plane(here)))
        return out

    stage = {(u, j): plane_stage(u, j) for u in range(UNITS) for j in range(nb)}

    def lead_indices(depth):
        out = [()]
        for _ in range(depth):
            out = [t + (b,) for t in out for b in range(2)]
        return out

    def plane_add(u, j):
        slot = u % SLOTS
        wait_all(stage[u, j])
        step = min(R, 64)
        for arr in range(2):
            order = L.order(arr)
            done = order[: j + 1]
            rest = sorted(order[j + 1 :])
            for lead in lead_indices(len(rest)):
                idx = [None] * nb
                for i in done:
                    idx[i] = L.bits[i]
                for i, b in zip(rest, lead):
                    idx[i] = b
                target = ring.at[(slot, arr) + tuple(idx)]
                source = recv[j].at[(u % 2, arr) + lead]

                @pl.loop(0, R // step)
                def _(r):
                    total = target[rows(r, step)].astype(F32) + source[rows(r, step)].astype(F32)
                    target[rows(r, step)] = total.astype(BF)

    ZC = HALF // mlp
    cols_of = lambda w: pl.ds(aligned(w * ZC, ZC), ZC)

    def z_scatter(u):
        out = []
        for arr in range(2):
            for o in range(1, mlp):
                there = lax.rem(z + o, mlp)
                src = ring.at[(u % SLOTS, arr) + my + (slice(None), cols_of(there))]
                out.append(L.copy(src, zr.at[u, o - 1, arr], L.along(o)))
        return out

    def z_gather(u):
        out = []
        for arr in range(2):
            view = G.at[(u, arr) + my + (slice(None), cols_of(z))]
            for o in range(1, mlp):
                out.append(L.copy(fin.at[u, arr], view, L.along(o)))
        return out

    def g_plane(u, j):
        out = []
        for arr in range(2):
            order = L.order(arr)
            view = G.at[(u, arr) + L.at(order[: j + 1], None, None)]
            out.append(L.copy(view, view, L.plane(order[j])))
        return out

    def attention_chain(u):
        scatter, back = z_scatter(u), z_gather(u)
        plane = [g_plane(u, j) for j in reversed(range(nb))]
        across = [L.copy(G.at[u], Gs.at[u], L.sibling())]
        kept = [make(fin.at[u, arr], G.at[(u, arr) + my + (slice(None), cols_of(z))]) for arr in range(2)]

        def z_sum():
            wait_all(scatter)
            for arr in range(2):
                total = ring[(u % SLOTS, arr) + my + (slice(None), cols_of(z))].astype(F32)
                for o in range(mlp - 1):
                    total = total + zr[u, o, arr].astype(F32)
                fin[u, arr] = total.astype(BF)

        begin = [functools.partial(start_all, stage[u, j]) for j in range(nb)]
        begin += [functools.partial(start_all, s) for s in [scatter, back + kept] + plane + [across]]
        end = [functools.partial(plane_add, u, j) for j in range(nb)] + [z_sum]
        end += [functools.partial(wait_all, s) for s in [back + kept] + plane + [across]]
        marks = {0: 0, 1: nb // 2, 2: nb, 3: nb + 1, 4: nb + 2, 5: nb + 2 + nb // 2, 6: 2 * nb + 2, 7: 2 * nb + 3}
        return Chain(begin, end, marks)

    def slice_grads_chain(k):
        u = k + 2
        begin = [functools.partial(start_all, stage[u, j]) for j in range(nb)]
        end = [functools.partial(plane_add, u, j) for j in range(nb)]
        if k < mlp - 1:
            sends = [L.copy(ring.at[(u % SLOTS, arr) + my], zf.at[k, arr], L.along(1 + k)) for arr in range(2)]
            begin.append(functools.partial(start_all, sends))
            end.append(functools.partial(wait_all, sends))
        return Chain(begin, end, {0: 0, 1: nb // 2, 2: nb, 3: nb + 1})

    U = [attention_chain(u) for u in range(2)]
    FG = [slice_grads_chain(k) for k in range(mlp)]
    W = slice_chain

    W[1].to(0)
    len_load.wait()
    tok_load.wait()

    @pl.loop(0, ROW // QB)
    def _(r):
        xhat, _ = layer_norm(n[rows(r, QB)].astype(F32))
        normed = (xhat * gain[...] + bias[...]).astype(BF)
        n[rows(r, QB)] = normed
        nT[:, rows(r, QB)] = jnp.transpose(normed)

    tok_swap.wait()

    @pl.loop(ROW // QB, 2 * ROW // QB)
    def _(r):
        xhat, _ = layer_norm(n[rows(r, QB)].astype(F32))
        normed = (xhat * gain[...] + bias[...]).astype(BF)
        n[rows(r, QB)] = normed
        nT[:, rows(r, QB)] = jnp.transpose(normed)

    g_load.wait()
    g_swap.wait()

    @pl.loop(0, 2 * ROW // QB)
    def _(r):
        gT[:, rows(r, QB)] = jnp.transpose(g[rows(r, QB)])

    len_swap.wait()
    wait_all(w_loads)
    lane_low = lax.broadcasted_iota(jnp.int32, (1, 128), 1) < HD

    heads = hid

    def attention(tables, mask, qs, ks, vs, ghs, gkT, gvT):
        for row in range(2):
            for k, t in enumerate(rotary_tables(lens, row, rates[...])):
                tables[row, k] = t
            for i in range(ROW // QB):
                lo, hi = band(i)
                query = lax.broadcasted_iota(jnp.int32, (QB, 128), 0) + i * QB
                start = doc_start(lens, row, query)
                for j in range(lo, hi, 128):
                    key = lax.broadcasted_iota(jnp.int32, (QB, 128), 1) + j
                    allowed = (key >= start) & (key <= query)
                    at = MASK_AT[i] + j - lo
                    mask[row, :, at : at + 128] = jnp.where(allowed, 0.0, -1e30)

        def attend(row, pair, col):
            out_cols = pl.ds(col, 128)
            gkT[...] = jnp.zeros_like(gkT)
            gvT[...] = jnp.zeros_like(gvT)
            for i in range(ROW // QB):
                lo, hi = band(i)
                width = hi - lo
                qb = qs[pair, i * QB : (i + 1) * QB]
                gb = ghs[pair, i * QB : (i + 1) * QB]
                kb, vb = ks[pair, lo:hi], vs[pair, lo:hi]
                hidden = mask[row, :, MASK_AT[i] : MASK_AT[i] + width]
                heads_pair, gq_pair = [], []
                for h in range(2):
                    mine = lane_low if h == 0 else ~lane_low
                    qm = jnp.where(mine, qb, jnp.zeros_like(qb))
                    gm = jnp.where(mine, gb, jnp.zeros_like(gb))
                    scores = nt(qm, kb) + hidden
                    exponent = jnp.exp(scores - jnp.max(scores, axis=-1, keepdims=True))
                    low = exponent.astype(BF)
                    mixed = nn(low, jnp.where(mine, vb, jnp.ones_like(vb)))
                    inverse = 1.0 / jnp.where(mine, pltpu.roll(mixed, 64, 1), mixed)
                    head = mixed * inverse
                    grad_w = nt(gm, vb)
                    centre = jnp.sum(gm.astype(F32) * head, axis=-1, keepdims=True)
                    grad_raw = (exponent * (grad_w - centre)).astype(BF)
                    gq_pair.append(nn(grad_raw, kb) * inverse)
                    gkT[:, lo:hi] += tn((qm.astype(F32) * inverse).astype(BF), grad_raw)
                    gvT[:, lo:hi] += tn((gm.astype(F32) * inverse).astype(BF), low)
                    heads_pair.append(head)
                here = pl.ds(aligned(row * ROW + i * QB, QB), QB)
                heads[here, out_cols] = jnp.where(lane_low, *heads_pair).astype(BF)
                gq = jnp.where(lane_low, *gq_pair) * (HD**-0.5)
                t = [tables[row, k, i * QB : (i + 1) * QB] for k in range(3)]
                gj[here, out_cols] = rotate_back(gq, *t).astype(BF)
            for i in range(ROW // QB):
                here = pl.ds(aligned(row * ROW + i * QB, QB), QB)
                t = [tables[row, k, i * QB : (i + 1) * QB] for k in range(3)]
                gk = jnp.transpose(gkT[:, i * QB : (i + 1) * QB])
                gj[here, pl.ds(aligned(HALF + col, 128), 128)] = rotate_back(gk, *t).astype(BF)
                gv = jnp.transpose(gvT[:, i * QB : (i + 1) * QB])
                gj[here, pl.ds(aligned(2 * HALF + col, 128), 128)] = gv.astype(BF)

        PB = 512

        def project(group, row):
            gcol = aligned(group * 256, 256)

            @pl.loop(0, ROW // PB)
            def _(r):
                here = pl.ds(aligned(row * ROW + r * PB, PB), PB)
                inside = rows(r, PB)
                nb_, gb = n[here], g[here]
                t = [tables[row, k, inside] for k in range(3)]
                block = lambda part: wup[(part,) + every + (slice(None), pl.ds(gcol, 256))].reshape(D, 256)
                q, k, v = [nn(nb_, block(part)) for part in range(3)]
                gh = nt(gb, wout_rows(group))
                for p in range(2):
                    cut = slice(p * 128, p * 128 + 128)
                    qs[p, inside] = rotate(q[:, cut], *t).astype(BF) * jnp.asarray(HD**-0.5, BF)
                    ks[p, inside] = rotate(k[:, cut], *t).astype(BF)
                    vs[p, inside] = v[:, cut].astype(BF)
                    ghs[p, inside] = gh[:, cut].astype(BF)

        def wout_rows(group):
            return wdown[(0, group)].reshape(256, D)

        def group_grads(u):
            gcol = u * 256

            @pl.loop(0, places)
            def _(p):
                here = rows(p, R)
                idx = L.place(p)
                for part in range(3):
                    arr, at = part // 2, (part % 2) * 256
                    lo = part * HALF + gcol
                    ring[(u, arr) + idx + (slice(None), pl.ds(at, 256))] = nn(nT[here], gj[:, lo : lo + 256]).astype(BF)
                ring[(u, 1) + idx + (slice(None), pl.ds(256, 256))] = nn(gT[here], heads[:, gcol : gcol + 256]).astype(BF)

        def after(step):
            if step == 3:
                group_grads(0)
            if step == 7:
                group_grads(1)
            for chain, mark in STEP_PLAN[step]:
                {"W": W, "U": U}[chain[0]][int(chain[1])].to(mark)

        @pl.loop(0, 8)
        def _(step):
            group, row, pair = step // 4, lax.rem(step // 2, 2), lax.rem(step, 2)

            @pl.when(pair == 0)
            def _():
                project(group, row)

            attend(row, pair, aligned(step // 4 * 256 + pair * 128, 128))

            for t in range(8):

                @pl.when(step == t)
                def _():
                    after(t)


    V = pltpu.VMEM
    pl.run_scoped(
        attention,
        V((2, 3, ROW, 128), F32),
        V((2, QB, MASK_AT[4]), F32),
        *[V((2, ROW, 128), BF)] * 4,
        *[V((128, ROW), F32)] * 2,
    )

    def feed_forward(acc_r, acc_g):
        blocks = 2 * ROW // QB
        gup = gj.at[:, pl.ds(0, HALF)]

        up_slot = lambda k: (3, 0, 1, 2)[k % 4]
        down_slot = lambda k: (k + 1) % 2

        def weights_in(k):
            if k == mlp - 1:
                return [
                    local(w_up.at[every + (slice(None), half_cols)], wup.at[up_slot(k)]),
                    local(w_down.at[core], wdown.at[down_slot(k)]),
                ]
            s = lax.rem(z + 1 + k, mlp)
            return [local(up_all.at[s], wup.at[up_slot(k)]), local(down_all.at[s], wdown.at[down_slot(k)])]

        W[1].to(3)
        pending = weights_in(0)

        @pl.loop(0, blocks)
        def _(r):
            acc_r[rows(r, QB)] = nn(hid[rows(r, QB)], wdown[0].reshape(HALF, D))
            total = nt(gj[rows(r, QB), pl.ds(0, HALF)], wup[0].reshape(D, HALF))
            for part in range(1, 3):
                total += nt(gj[rows(r, QB), pl.ds(part * HALF, HALF)], wup[part].reshape(D, HALF))
            acc_g[rows(r, QB)] = total

        def advance(k, where):
            for chain, mark in SLICE_PLAN.get((min(k, mlp - 1), where), ()):
                {"W": W, "U": U, "F": FG}[chain[0]][int(chain[1])].to(mark)

        advance(0, "init")

        swap_r = L.copy(gj.at[pl.ds(0, ROW), pl.ds(HALF, D)], n.at[sib], L.sibling())
        swap_g = L.copy(gj.at[pl.ds(ROW, ROW), pl.ds(HALF, D)], g.at[sib], L.sibling())

        for k in range(mlp):
            last = k == mlp - 1
            wait_all(pending)
            if not last:
                if k + 1 < mlp - 1:
                    W[k + 2].to(3)
                pending = weights_in(k + 1)
            us, ds = up_slot(k), down_slot(k)

            def token_block(r):
                here = rows(r, QB)
                w1, w2 = wup[us].reshape(D, HALF), wdown[ds].reshape(HALF, D)
                up = nn(n[here], w1)
                hidden, slope = gelu_and_slope(up)
                hidden = hidden.astype(BF)
                hid[here] = hidden
                acc_r[here] += nn(hidden, w2)
                grad = (nt(g[here], w2) * slope).astype(BF)
                gup[here] = grad
                acc_g[here] += nt(grad, w1)

            pl.loop(0, blocks // 2, unroll=2)(token_block)
            advance(k, "mid")
            pl.loop(blocks // 2, blocks, unroll=2)(token_block)
            if last:
                pl.semaphore_signal(free_sem, inc=1, device_id=L.sibling(), device_id_type=MESH)
                tok_again = local(tokens, n.at[own])

                @pl.loop(0, ROW // QB)
                def _(r):
                    there = pl.ds(aligned(ROW + r * QB, QB), QB)
                    gj[rows(r, QB), pl.ds(HALF, D)] = acc_r[there].astype(BF)
                    gj[there, pl.ds(HALF, D)] = acc_g[there].astype(BF)

                pl.semaphore_wait(free_sem, 1)
                start_all([swap_r, swap_g])
            advance(k, "tokens")
            slot = (k + 2) % SLOTS
            if k >= SLOTS:
                FG[k - SLOTS].to(3)

            @pl.loop(0, places)
            def _(p):
                ring[(slot, 0) + L.place(p)] = nn(nT[rows(p, R)], gup[...]).astype(BF)

            advance(k, "up")

            @pl.loop(0, places)
            def _(p):
                ring[(slot, 1) + L.place(p)] = nn(gT[rows(p, R)], hid[...]).astype(BF)

            FG[k].to(0)
            advance(k, "down")

        tok_again.wait()
        swap_r.wait()
        swap_g.wait()
        sum_send[0] = jnp.zeros_like(sum_send[0])
        FB = 128

        @pl.loop(0, ROW // FB)
        def _(r):
            here = rows(r, FB)
            there = pl.ds(aligned(ROW + r * FB, FB), FB)
            x = n[here].astype(F32)
            xhat, inverse = layer_norm(x)
            n[here] = (x + acc_r[here] + n[there].astype(F32)).astype(BF)
            grad = acc_g[here] + g[there].astype(F32)
            sum_send[0, 0:1] += jnp.sum(grad * xhat, axis=0, keepdims=True)
            sum_send[0, 1:2] += jnp.sum(grad, axis=0, keepdims=True)
            scaled = grad * gain[...]
            acc_g[here] = g[here].astype(F32) + inverse * (
                scaled
                - jnp.mean(scaled, axis=-1, keepdims=True)
                - xhat * jnp.mean(scaled * xhat, axis=-1, keepdims=True)
            )

        outs = [local(n.at[own], result), local(acc_g.at[pl.ds(0, ROW)], d_tokens)]

        partners = L.pairs()
        adds = [L.copy(sum_send.at[i], sum_recv.at[i], device) for i, device in enumerate(partners)]

        def sum_step(i):
            adds[i].wait()
            sum_send[i + 1] = sum_send[i] + sum_recv[i]
            if i + 1 < len(adds):
                adds[i + 1].start()

        adds[0].start()
        sum_step(0)
        u = mlp + 1
        final = FG[mlp - 1]
        final.to(1)
        if len(adds) > 1:
            sum_step(1)
        if len(adds) > 2:
            sum_step(2)
        final.to(2)
        for i in range(mlp - 1):
            FG[i].to(3)
        slot = u % SLOTS
        S = R // 2
        for arr in range(2):
            for keep in range(2):
                lo = pl.ds(aligned((core if keep else 1 - core) * S, S), S)
                total = ring[(slot, arr) + my + (lo,)].astype(F32)
                for i in range(mlp - 1):
                    total = total + zf[i, arr, lo].astype(F32)
                if keep:
                    (up_st if arr == 0 else down_st)[0] = total
                else:
                    swap_out[arr] = total.astype(BF)
        last_swap = L.copy(swap_out, swap_in, L.sibling())
        last_swap.start()
        for i in range(3, len(adds)):
            sum_step(i)
        sums_out[...] = sum_send[len(adds)]
        U[0].to(7)
        U[1].to(7)
        last_swap.wait()
        up_st[1] = swap_in[0].astype(F32)
        down_st[1] = swap_in[1].astype(F32)
        for i in range(2):
            which = core if i == 0 else 1 - core
            outs.append(local(up_st.at[i], d_up.at[:, pl.ds(aligned(which * HALF, HALF), HALF)]))
            outs.append(local(down_st.at[i], d_down.at[:, pl.ds(aligned(which * HALF, HALF), HALF)]))
        wait_all(outs)

    pl.run_scoped(feed_forward, V((2 * ROW, D), F32), V((2 * ROW, D), F32))


CB = 128


def convert_kernel(mine, theirs, res_in, tok_in, sums, up_in, down_in, d_qkv, d_out, result, d_tokens, d_gain, d_bias, d_up, d_down):
    core = lax.rem(lax.axis_index("dp"), 2)
    result[...] = res_in[...]
    d_tokens[...] = tok_in[...]
    for who, ref in ((core, mine), (1 - core, theirs)):
        for u in range(2):
            lane = who * HALF + u * 256
            for part in range(3):
                at = (part % 2) * 256
                d_qkv[:, pl.ds(aligned(part * D + lane, 256), 256)] = ref[u, part // 2, :, at : at + 256].astype(F32)
            d_out[pl.ds(aligned(lane, 256), 256)] = jnp.transpose(ref[u, 1, :, 256:].astype(F32))

    @pl.when(pl.program_id(0) == 0)
    def _():
        d_gain[...] = sums[0:1]
        d_bias[...] = sums[1:2]
        d_up[...] = up_in[...]
        if d_down.shape == down_in.shape:
            d_down[...] = down_in[...]
        else:
            d_down[...] = jnp.transpose(down_in[...])


def convert(mine, theirs, *rest):
    S = jax.ShapeDtypeStruct
    block = pl.BlockSpec((2, 2, CB, HALF), lambda r: (0, 0, r, 0))
    rows_of = pl.BlockSpec((CB, D), lambda r: (r, 0))
    whole = lambda *s: pl.BlockSpec(s, lambda r: (0, 0))
    size = rest[3].shape[0]
    turned = (D, size) if size % 128 == 0 else (size, D)
    *outs, d_down = pl.pallas_call(
        convert_kernel,
        grid=(D // CB,),
        out_shape=[
            S((D, 3 * D), F32), S((D, D), F32), S((ROW, D), BF), S((ROW, D), F32),
            S((1, D), F32), S((1, D), F32), S((size, D), F32), S(turned, F32),
        ],
        in_specs=[block, block, rows_of, rows_of, whole(8, D), whole(size, D), whole(size, D)],
        out_specs=[
            pl.BlockSpec((CB, 3 * D), lambda r: (r, 0)), pl.BlockSpec((D, CB), lambda r: (0, r)), rows_of, rows_of,
            whole(1, D), whole(1, D), whole(size, D), whole(*turned),
        ],
        cost_estimate=pl.CostEstimate(flops=10**7, bytes_accessed=36 * MiB, transcendentals=0),
        compiler_params=pltpu.CompilerParams(vmem_limit_bytes=48 * MiB),
        name="convert",
    )(mine, theirs, *rest)
    return (*outs, d_down if turned == (D, size) else d_down.T)


def shards(dp, mlp, tokens, gain, bias, w_qkv, w_out, w_up, w_down, lengths, grad_out):
    nb = (dp // 2).bit_length() - 1
    places = 1 << nb
    bits, R, Rd = (2,) * nb, D // places, HALF // places
    slots = 3
    rates = jnp.exp(jnp.arange(8).astype(F32) * (-2.0 * math.log(10000.0) / 16)).reshape(8, 1)
    anyspec, vm = pl.BlockSpec(memory_space=pl.ANY), pl.BlockSpec(memory_space=pltpu.VMEM)
    S = jax.ShapeDtypeStruct
    V = pltpu.VMEM
    two = 2 * ROW
    steps = nb + mlp.bit_length()
    gathered = (2, 2) + bits + (R, HALF)
    out_shape = [
        S((ROW, D), BF), S((ROW, D), F32), S((8, D), F32), S((R // 2, D), F32), S((R // 2, D), F32),
        S(gathered, BF), S(gathered, BF), S((mlp,) + bits + (R, HALF), BF), S((mlp,) + bits + (Rd, D), BF),
    ]
    out_specs = [anyspec] * 9
    out_specs[2] = vm
    outs = pl.pallas_call(
        functools.partial(whole_kernel, dp, mlp),
        out_shape=out_shape,
        in_specs=[anyspec, vm, vm, vm] + [anyspec] * 6,
        out_specs=out_specs,
        scratch_shapes=[
            V((two, D), BF), V((D, two), BF), V((two, D), BF), V((D, two), BF),
            V((4,) + bits + (R, HALF), BF), V((2,) + bits + (Rd, D), BF),
            V((slots, 2) + bits + (R, HALF), BF),
            [V((2, 2) + (2,) * (nb - 1 - j) + (R, HALF), BF) for j in range(nb)],
            V((2, mlp - 1, 2, R, HALF // mlp), BF), V((2, 2, R, HALF // mlp), BF), V((mlp - 1, 2, R, HALF), BF),
            V((2, R // 2, HALF), BF), V((2, R // 2, HALF), BF),
            V((2, 8, 128), jnp.int32), V((steps + 1, 8, D), F32), V((steps, 8, D), F32),
            V((2, R // 2, HALF), F32), V((2, R // 2, HALF), F32),
            V((two, HALF), BF), V((two, 3 * HALF), BF),
            pltpu.SemaphoreType.DMA((192,)), pltpu.SemaphoreType.DMA((192,)), pltpu.SemaphoreType.DMA((64,)),
            pltpu.SemaphoreType.REGULAR,
        ],
        compiler_params=pltpu.CompilerParams(vmem_limit_bytes=63 * MiB, collective_id=0, has_side_effects=True),
        cost_estimate=pl.CostEstimate(flops=120 * 10**9, bytes_accessed=60 * MiB, transcendentals=0),
        name="block",
    )(
        jnp.pad(lengths, ((0, 7), (0, 120))), rates, gain.reshape(1, D), bias.reshape(1, D), tokens, grad_out,
        w_qkv.reshape(bits + (R, 3 * D)), w_out.reshape((2,) + bits + (Rd, D)),
        w_up.reshape(bits + (R, D)), w_down.reshape((2,) + bits + (Rd, D)),
    )
    result, d_tokens, sums, d_up, d_down, mine, theirs = outs[:7]
    d_qkv, d_out, result, d_tokens, d_gain, d_bias, d_up, d_down = convert(
        mine.reshape(2, 2, D, HALF), theirs.reshape(2, 2, D, HALF), result, d_tokens, sums, d_up, d_down
    )
    return (result, d_tokens, d_gain.reshape(D), d_bias.reshape(D), d_qkv, d_out, d_up, d_down)


def solution(mesh):
    dp, mlp = mesh.shape["dp"], mesh.shape["mlp"]
    rows_in = P(("dp", "mlp"), None)
    in_specs = (rows_in, P(), P(), P(), P(), P(None, "mlp"), P("mlp", None), rows_in, rows_in)
    out_specs = (rows_in, rows_in, P(), P(), P(), P(), P("dp", "mlp"), P("mlp", "dp"))
    body = functools.partial(shards, dp, mlp)
    return jax.shard_map(body, mesh=mesh, in_specs=in_specs, out_specs=out_specs, check_vma=False)
```

```python
import functools
import math

import jax
import jax.numpy as jnp
from jax import lax
from jax.experimental import pallas as pl
from jax.experimental.pallas import tpu as pltpu
from jax.sharding import PartitionSpec as P

D = 1024
HD = 64
ROW = 1024
EPSILON = 1e-05
ROOT_HALF = 0.7071067811865476
NORMAL_PEAK = 0.3989422804014327
BF = jnp.bfloat16
F32 = jnp.float32
QB = 256
HALF = D // 2
MiB = 1 << 20
MESH = pl.DeviceIdType.MESH


def nn(a, b):
    return lax.dot_general(a, b, (((1,), (0,)), ((), ())), preferred_element_type=F32)


def nt(a, b):
    return lax.dot_general(a, b, (((1,), (1,)), ((), ())), preferred_element_type=F32)


def tn(a, b):
    return lax.dot_general(a, b, (((0,), (0,)), ((), ())), preferred_element_type=F32)


def layer_norm(x):
    mean = jnp.mean(x, axis=-1, keepdims=True)
    centered = x - mean
    var = jnp.mean(centered * centered, axis=-1, keepdims=True)
    inverse = lax.rsqrt(var + EPSILON)
    return centered * inverse, inverse


def doc_start(lengths, row, places):
    start = jnp.zeros_like(places)
    end = jnp.zeros((1, 1), jnp.int32)
    for d in range(8):
        end = end + lengths[row, 0:1, d : d + 1]
        start = jnp.where(places >= end, end, start)
    return start


def rotary_tables(lengths, row, rates):
    places = lax.broadcasted_iota(jnp.int32, (8, ROW), 1)
    pos = places - doc_start(lengths, row, places)
    angles = pos.astype(F32) * rates
    cosine, sine = jnp.cos(angles), jnp.sin(angles)
    ones, zeros = jnp.ones((48, ROW), F32), jnp.zeros((8, ROW), F32)
    pad = jnp.zeros((48, ROW), F32)
    table = lambda *parts: jnp.transpose(jnp.concatenate(parts * 2, axis=0))
    return (
        table(cosine, cosine, ones),
        table(-sine, zeros, pad),
        table(zeros, sine, pad),
    )


def rotate(x, cosine, sine_a, sine_b):
    return x * cosine + pltpu.roll(x, 120, 1) * sine_a + pltpu.roll(x, 8, 1) * sine_b


def rotate_back(x, cosine, sine_a, sine_b):
    return x * cosine - pltpu.roll(x, 120, 1) * sine_a - pltpu.roll(x, 8, 1) * sine_b


def band(i):
    return max(0, i - 2) * QB, (i + 1) * QB


MASK_AT = [sum(band(k)[1] - band(k)[0] for k in range(i)) for i in range(5)]


ERFC_RATE = 0.55 * ROOT_HALF
ERFC_TERMS = (
    0.30159098847742044, 0.3907933818624623, -0.04130162875264046,
    0.7595567015262069, -0.5179392414738552, 0.10729981475108823,
)


def gelu_and_slope(u):
    density = jnp.exp(-0.5 * u * u)
    t = pltpu.reciprocal(1.0 + ERFC_RATE * jnp.abs(u))
    poly = 0.5 * ERFC_TERMS[5]
    for term in ERFC_TERMS[4::-1]:
        poly = poly * t + 0.5 * term
    tail = poly * t * density
    bell = jnp.where(u < 0.0, tail, 1.0 - tail)
    return u * bell, bell + u * density * NORMAL_PEAK


def aligned(start, unit):
    return pl.multiple_of(start, unit)


def rows(r, size):
    return pl.ds(aligned(r * size, size), size)
STEP_PLAN = {
    (0, False): (("W1", 1), ("W2", 0)),
    (0, True): (("W1", 2),),
    (2, False): (("W1", 3), ("W2", 1), ("W3", 0)),
    (3, False): (("W2", 2),),
    (3, True): (("U0", 0),),
    (5, False): (("U0", 1), ("W2", 3)),
    (5, True): (("W3", 1),),
    (6, False): (("U0", 2),),
    (6, True): (("W3", 2),),
    (7, False): (("U0", 3),),
    (7, True): (("U1", 0), ("U0", 4)),
}
SLICE_PLAN = {
    (0, "tokens"): (("U1", 1), ("U0", 5)),
    (1, "mid"): (("U1", 2),),
    (1, "tokens"): (("F0", 1),),
    (1, "down"): (("U1", 3), ("U0", 6)),
    (2, "mid"): (("F0", 2),),
    (2, "tokens"): (("F1", 1), ("U1", 4)),
    (2, "down"): (("U1", 5),),
    (3, "mid"): (("F1", 2),),
    (3, "tokens"): (("F2", 1), ("U1", 6)),
    (3, "down"): (("F2", 2),),
    (3, "own"): (("F3", 1),),
}


class Links:
    def __init__(self, dp, mlp, send_sems, recv_sems):
        self.nb, self.mlp = (dp // 2).bit_length() - 1, mlp
        self.d, self.z = lax.axis_index("dp"), lax.axis_index("mlp")
        self.core = lax.rem(self.d, 2)
        self.bits = [self.bit(self.d, 2 << (self.nb - 1 - i)) for i in range(self.nb)]
        self.send_sems, self.recv_sems, self.count = send_sems, recv_sems, 0

    @staticmethod
    def bit(index, weight):
        return lax.rem(index // weight, 2)

    def flip(self, index, weight):
        return index + weight * (1 - 2 * self.bit(index, weight))

    def sibling(self):
        return (self.flip(self.d, 1), self.z)

    def plane(self, i):
        return (self.flip(self.d, 2 << (self.nb - 1 - i)), self.z)

    def along(self, offset):
        return (self.d, lax.rem(self.z + offset, self.mlp))

    def pairs(self):
        out = [self.sibling()] + [self.plane(i) for i in range(self.nb)]
        return out + [(self.d, self.flip(self.z, 1 << b)) for b in range(self.mlp.bit_length() - 1)]

    def copy(self, src, dst, device):
        k, self.count = self.count, self.count + 1
        return pltpu.make_async_remote_copy(
            src_ref=src,
            dst_ref=dst,
            send_sem=self.send_sems.at[k],
            recv_sem=self.recv_sems.at[k],
            device_id=device,
            device_id_type=MESH,
        )

    def order(self, arr):
        return list(range(self.nb)) if arr == 0 else list(range(self.nb))[::-1]

    def at(self, done, current, value):
        out = [slice(None)] * self.nb
        for i in done:
            out[i] = self.bits[i]
        if current is not None:
            out[current] = value
        return tuple(out)

    def place(self, p):
        return tuple(lax.rem(p // (1 << (self.nb - 1 - i)), 2) for i in range(self.nb))

    def mine(self):
        return tuple(self.bits)


def start_all(copies):
    for copy in copies:
        copy.start()
    return copies


def start_split(core, copies):
    @pl.when(core == 0)
    def _():
        start_all(copies)

    @pl.when(core == 1)
    def _():
        start_all(copies[::-1])


def wait_all(copies):
    for copy in copies:
        copy.wait()


class Chain:
    def __init__(self, begin, end, marks):
        self.begin, self.end, self.marks, self.at = begin, end, marks, -1

    def to(self, mark):
        goal = self.marks[mark]
        while self.at < goal:
            if self.at >= 0:
                self.end[self.at]()
            self.at += 1
            if self.at < len(self.begin):
                self.begin[self.at]()


def whole_kernel(
    dp, mlp,
    len_own, rates, gain, bias, tokens, grad_out, w_qkv, w_out, w_up, w_down,
    result, d_tokens, sums_out, d_up, d_down, G, Gs, up_all, down_all, heads_out, gj_out,
    n, nT, g, gT, wup, wdown, ring, recv, zr, fin, zf, swap_out, swap_in, lens, sum_send, sum_recv,
    hid, gj,
    send_sems, recv_sems, sems, free_sem,
):
    L = Links(dp, mlp, send_sems, recv_sems)
    nb, core, z = L.nb, L.core, L.z
    places = 1 << nb
    R = D // places

    barrier = pltpu.get_barrier_semaphore()
    greeted = [L.sibling()] + [L.plane(i) for i in range(nb)] + [L.along(o) for o in range(1, mlp)]
    for device in greeted:
        pl.semaphore_signal(barrier, inc=1, device_id=device, device_id_type=MESH)
    pl.semaphore_wait(barrier, len(greeted))

    used = [0]

    def make(src, dst):
        k, used[0] = used[0], used[0] + 1
        return pltpu.make_async_copy(src, dst, sems.at[k])

    def local(src, dst):
        copy = make(src, dst)
        copy.start()
        return copy

    own, sib = pl.ds(0, ROW), pl.ds(ROW, ROW)
    half_cols = pl.ds(aligned(core * HALF, HALF), HALF)
    every = (slice(None),) * nb

    len_swap = L.copy(len_own, lens.at[1], L.sibling())
    tok_swap = L.copy(tokens, n.at[sib], L.sibling())
    g_swap = L.copy(grad_out, g.at[sib], L.sibling())
    start_all([len_swap, tok_swap])
    tok_load = local(tokens, n.at[own])
    len_load = local(len_own, lens.at[0])
    g_swap.start()
    g_load = local(grad_out, g.at[own])
    w_loads = []
    for part in range(3):
        cols = pl.ds(aligned(part * D + core * HALF, HALF), HALF)
        w_loads.append(local(w_qkv.at[every + (slice(None), cols)], wup.at[part]))
    w_loads.append(local(w_out.at[core], wdown.at[0]))

    my = L.mine()

    def gather(o):
        there = lax.rem(z + o, mlp)
        stages = [
            [
                L.copy(w_up.at[my + (slice(None), half_cols)], up_all.at[(z,) + my], L.along(mlp - o)),
                L.copy(w_down.at[(core,) + my], down_all.at[(z,) + my], L.along(mlp - o)),
            ]
        ]
        for j in reversed(range(nb)):
            copies = []
            for arr, ref in enumerate((up_all, down_all)):
                order = L.order(arr)
                view = ref.at[(there,) + L.at(order[: j + 1], None, None)]
                copies.append(L.copy(view, view, L.plane(order[j])))
            stages.append(copies)
        marks = {0: 0, 1: 1, 2: 1 + nb // 2, 3: 1 + nb}
        return Chain(
            [functools.partial(start_all, stages[0])] + [functools.partial(start_split, core, s) for s in stages[1:]],
            [functools.partial(wait_all, s) for s in stages],
            marks,
        )

    slice_chain = [None] + [gather(o) for o in range(1, mlp)]

    UNITS = 2 + mlp
    SLOTS = ring.shape[0]

    def plane_stage(u, j):
        slot, out = u % SLOTS, []
        for arr in range(2):
            order = L.order(arr)
            here = order[j]
            src = ring.at[(slot, arr) + L.at(order[:j], here, 1 - L.bits[here])]
            out.append(L.copy(src, recv[j].at[u % 2, arr], L.plane(here)))
        return out

    stage = {(u, j): plane_stage(u, j) for u in range(UNITS) for j in range(nb)}

    def lead_indices(depth):
        out = [()]
        for _ in range(depth):
            out = [t + (b,) for t in out for b in range(2)]
        return out

    def plane_add(u, j):
        slot = u % SLOTS
        wait_all(stage[u, j])
        step = min(R, 64)
        for arr in range(2):
            order = L.order(arr)
            done = order[: j + 1]
            rest = sorted(order[j + 1 :])
            for lead in lead_indices(len(rest)):
                idx = [None] * nb
                for i in done:
                    idx[i] = L.bits[i]
                for i, b in zip(rest, lead):
                    idx[i] = b
                target = ring.at[(slot, arr) + tuple(idx)]
                source = recv[j].at[(u % 2, arr) + lead]

                @pl.loop(0, R // step)
                def _(r):
                    total = target[rows(r, step)].astype(F32) + source[rows(r, step)].astype(F32)
                    target[rows(r, step)] = total.astype(BF)

    ZC = HALF // mlp
    cols_of = lambda w: pl.ds(aligned(w * ZC, ZC), ZC)

    def z_scatter(u):
        out = []
        for arr in range(2):
            for o in range(1, mlp):
                there = lax.rem(z + o, mlp)
                src = ring.at[(u % SLOTS, arr) + my + (slice(None), cols_of(there))]
                out.append(L.copy(src, zr.at[u, o - 1, arr], L.along(o)))
        return out

    def z_gather(u):
        out = []
        for arr in range(2):
            view = G.at[(u, arr) + my + (slice(None), cols_of(z))]
            for o in range(1, mlp):
                out.append(L.copy(fin.at[u, arr], view, L.along(o)))
        return out

    def g_plane(u, j):
        out = []
        for arr in range(2):
            order = L.order(arr)
            view = G.at[(u, arr) + L.at(order[: j + 1], None, None)]
            out.append(L.copy(view, view, L.plane(order[j])))
        return out

    def attention_chain(u):
        scatter, back = z_scatter(u), z_gather(u)
        plane = [g_plane(u, j) for j in reversed(range(nb))]
        across = [L.copy(G.at[u], Gs.at[u], L.sibling())]
        kept = [make(fin.at[u, arr], G.at[(u, arr) + my + (slice(None), cols_of(z))]) for arr in range(2)]

        def z_sum():
            wait_all(scatter)
            for arr in range(2):
                total = ring[(u % SLOTS, arr) + my + (slice(None), cols_of(z))].astype(F32)
                for o in range(mlp - 1):
                    total = total + zr[u, o, arr].astype(F32)
                fin[u, arr] = total.astype(BF)

        begin = [functools.partial(start_split, core, stage[u, j]) for j in range(nb)]
        begin += [functools.partial(start_all, s) for s in (scatter, back + kept)]
        begin += [functools.partial(start_split, core, s) for s in plane] + [functools.partial(start_all, across)]
        end = [functools.partial(plane_add, u, j) for j in range(nb)] + [z_sum]
        end += [functools.partial(wait_all, s) for s in [back + kept] + plane + [across]]
        marks = {0: 0, 1: nb // 2, 2: nb, 3: nb + 1, 4: nb + 2, 5: nb + 2 + nb // 2, 6: 2 * nb + 2, 7: 2 * nb + 3}
        return Chain(begin, end, marks)

    def slice_grads_chain(k):
        u = k + 2
        begin = [functools.partial(start_split, core, stage[u, j]) for j in range(nb)]
        end = [functools.partial(plane_add, u, j) for j in range(nb)]
        if k < mlp - 1:
            sends = [L.copy(ring.at[(u % SLOTS, arr) + my], zf.at[k, arr], L.along(1 + k)) for arr in range(2)]
            begin.append(functools.partial(start_all, sends))
            end.append(functools.partial(wait_all, sends))
        return Chain(begin, end, {0: 0, 1: nb // 2, 2: nb, 3: nb + 1})

    U = [attention_chain(u) for u in range(2)]
    FG = [slice_grads_chain(k) for k in range(mlp)]
    W = slice_chain

    W[1].to(0)
    len_load.wait()
    tok_load.wait()

    @pl.loop(0, ROW // QB)
    def _(r):
        xhat, _ = layer_norm(n[rows(r, QB)].astype(F32))
        normed = (xhat * gain[...] + bias[...]).astype(BF)
        n[rows(r, QB)] = normed
        nT[:, rows(r, QB)] = jnp.transpose(normed)

    tok_swap.wait()

    @pl.loop(ROW // QB, 2 * ROW // QB)
    def _(r):
        xhat, _ = layer_norm(n[rows(r, QB)].astype(F32))
        normed = (xhat * gain[...] + bias[...]).astype(BF)
        n[rows(r, QB)] = normed
        nT[:, rows(r, QB)] = jnp.transpose(normed)

    g_load.wait()
    g_swap.wait()

    @pl.loop(0, 2 * ROW // QB)
    def _(r):
        gT[:, rows(r, QB)] = jnp.transpose(g[rows(r, QB)])

    len_swap.wait()
    wait_all(w_loads)
    lane_low = lax.broadcasted_iota(jnp.int32, (1, 128), 1) < HD

    heads = hid

    def group_saves(u):
        lanes = [pl.ds(part * HALF + u * 256, 256) for part in range(3)]
        return [make(gj.at[:, at], gj_out.at[:, at]) for at in lanes] + [make(hid.at[:, lanes[0]], heads_out.at[:, lanes[0]])]

    saves = [group_saves(u) for u in range(2)]

    def attention(tables, mask, qs, ks, vs, ghs, gkT, gvT):
        for row in range(2):
            for k, t in enumerate(rotary_tables(lens, row, rates[...])):
                tables[row, k] = t
            for i in range(ROW // QB):
                lo, hi = band(i)
                query = lax.broadcasted_iota(jnp.int32, (QB, 128), 0) + i * QB
                start = doc_start(lens, row, query)
                for j in range(lo, hi, 128):
                    key = lax.broadcasted_iota(jnp.int32, (QB, 128), 1) + j
                    allowed = (key >= start) & (key <= query)
                    at = MASK_AT[i] + j - lo
                    mask[row, :, at : at + 128] = jnp.where(allowed, 0.0, -1e30)

        def attend(row, pair, col, halfway):
            out_cols = pl.ds(col, 128)
            gkT[...] = jnp.zeros_like(gkT)
            gvT[...] = jnp.zeros_like(gvT)
            for i in range(ROW // QB):
                lo, hi = band(i)
                width = hi - lo
                qb = qs[pair, i * QB : (i + 1) * QB]
                gb = ghs[pair, i * QB : (i + 1) * QB]
                kb, vb = ks[pair, lo:hi], vs[pair, lo:hi]
                hidden = mask[row, :, MASK_AT[i] : MASK_AT[i] + width]
                stack = lambda x: jnp.concatenate(
                    [jnp.where(lane_low, x, jnp.zeros_like(x)), jnp.where(lane_low, jnp.zeros_like(x), x)]
                )
                q2, g2 = stack(qb), stack(gb)
                scores = nt(q2, kb) + jnp.concatenate([hidden, hidden])
                exponent = jnp.exp(scores - jnp.max(scores, axis=-1, keepdims=True))
                low = exponent.astype(BF)
                mixed = nn(low, jnp.concatenate([vb, jnp.ones_like(vb)], axis=1))
                inverse = 1.0 / mixed[:, 128:]
                head = mixed[:, :128] * inverse
                g2f = g2.astype(F32)
                centre = jnp.sum(g2f * head, axis=-1, keepdims=True)
                grad_raw = (exponent * (nt(g2, vb) - centre)).astype(BF)
                gq2 = nn(grad_raw, kb) * inverse
                gkT[:, lo:hi] += tn((q2.astype(F32) * inverse).astype(BF), grad_raw)
                gvT[:, lo:hi] += tn((g2f * inverse).astype(BF), low)
                heads_pair, gq_pair = (head[:QB], head[QB:]), (gq2[:QB], gq2[QB:])
                here = pl.ds(aligned(row * ROW + i * QB, QB), QB)
                heads[here, out_cols] = jnp.where(lane_low, *heads_pair).astype(BF)
                gq = jnp.where(lane_low, *gq_pair) * (HD**-0.5)
                t = [tables[row, k, i * QB : (i + 1) * QB] for k in range(3)]
                gj[here, out_cols] = rotate_back(gq, *t).astype(BF)
                if i == 2:
                    halfway()
            for i in range(ROW // QB):
                here = pl.ds(aligned(row * ROW + i * QB, QB), QB)
                t = [tables[row, k, i * QB : (i + 1) * QB] for k in range(3)]
                gk = jnp.transpose(gkT[:, i * QB : (i + 1) * QB])
                gj[here, pl.ds(aligned(HALF + col, 128), 128)] = rotate_back(gk, *t).astype(BF)
                gv = jnp.transpose(gvT[:, i * QB : (i + 1) * QB])
                gj[here, pl.ds(aligned(2 * HALF + col, 128), 128)] = gv.astype(BF)

        PB = 512

        def project(group, row):
            gcol = aligned(group * 256, 256)

            @pl.loop(0, ROW // PB)
            def _(r):
                here = pl.ds(aligned(row * ROW + r * PB, PB), PB)
                inside = rows(r, PB)
                nb_, gb = n[here], g[here]
                t = [tables[row, k, inside] for k in range(3)]
                block = lambda part: wup[(part,) + every + (slice(None), pl.ds(gcol, 256))].reshape(D, 256)
                q, k, v = [nn(nb_, block(part)) for part in range(3)]
                gh = nt(gb, wout_rows(group))
                for p in range(2):
                    cut = slice(p * 128, p * 128 + 128)
                    qs[p, inside] = rotate(q[:, cut], *t).astype(BF) * jnp.asarray(HD**-0.5, BF)
                    ks[p, inside] = rotate(k[:, cut], *t).astype(BF)
                    vs[p, inside] = v[:, cut].astype(BF)
                    ghs[p, inside] = gh[:, cut].astype(BF)

        def wout_rows(group):
            return wdown[(0, group)].reshape(256, D)

        def group_grads(u):
            gcol = u * 256

            @pl.loop(0, places)
            def _(p):
                here = rows(p, R)
                idx = L.place(p)
                for part in range(3):
                    arr, at = part // 2, (part % 2) * 256
                    lo = part * HALF + gcol
                    ring[(u, arr) + idx + (slice(None), pl.ds(at, 256))] = nn(nT[here], gj[:, lo : lo + 256]).astype(BF)
                ring[(u, 1) + idx + (slice(None), pl.ds(256, 256))] = nn(gT[here], heads[:, gcol : gcol + 256]).astype(BF)

        def after(step, late):
            if late and step in (3, 7):
                start_all(saves[step // 4])
                group_grads(step // 4)
            for chain, mark in STEP_PLAN.get((step, late), ()):
                {"W": W, "U": U}[chain[0]][int(chain[1])].to(mark)

        @pl.loop(0, 8)
        def _(step):
            group, row, pair = step // 4, lax.rem(step // 2, 2), lax.rem(step, 2)

            @pl.when(pair == 0)
            def _():
                project(group, row)

            def hooks(late):
                for t in range(8):
                    if STEP_PLAN.get((t, late)) or (late and t in (3, 7)):

                        @pl.when(step == t)
                        def _():
                            after(t, late)

            attend(row, pair, aligned(step // 4 * 256 + pair * 128, 128), lambda: hooks(False))
            hooks(True)

    V = pltpu.VMEM
    pl.run_scoped(
        attention,
        V((2, 3, ROW, 128), F32),
        V((2, QB, MASK_AT[4]), F32),
        *[V((2, ROW, 128), BF)] * 4,
        *[V((128, ROW), F32)] * 2,
    )

    def feed_forward(acc_r, acc_g):
        blocks, TB = 2 * ROW // QB, 512
        gup = gj.at[:, pl.ds(0, HALF)]

        up_slot = lambda k: (3, 0, 1, 2)[k % 4]
        down_slot = lambda k: (k + 1) % 2

        def weights_in(k):
            if k == mlp - 1:
                return [
                    local(w_up.at[every + (slice(None), half_cols)], wup.at[up_slot(k)]),
                    local(w_down.at[core], wdown.at[down_slot(k)]),
                ]
            s = lax.rem(z + 1 + k, mlp)
            return [local(up_all.at[s], wup.at[up_slot(k)]), local(down_all.at[s], wdown.at[down_slot(k)])]

        def advance(k, where):
            for chain, mark in SLICE_PLAN.get((min(k, mlp - 1), where), ()):
                {"W": W, "U": U, "F": FG}[chain[0]][int(chain[1])].to(mark)

        W[1].to(3)
        pending = weights_in(0)

        for save in saves:
            wait_all(save)

        swap_r = L.copy(nT.at[:, pl.ds(0, D)], n.at[sib], L.sibling())
        swap_g = L.copy(nT.at[:, pl.ds(D, D)], g.at[sib], L.sibling())
        used_up = [up_slot(k) for k in range(mlp - 1)]

        for k in range(mlp):
            last = k == mlp - 1
            wait_all(pending)
            if not last:
                if k + 1 < mlp - 1:
                    W[k + 2].to(3)
                pending = weights_in(k + 1)
            else:
                again = []
                for part in range(3):
                    cols = pl.ds(aligned(part * D + core * HALF, HALF), HALF)
                    again.append(local(w_qkv.at[every + (slice(None), cols)], wup.at[used_up[part]]))
                    if part:
                        lanes = pl.ds(part * HALF, HALF)
                        again.append(local(gj_out.at[:, lanes], gj.at[:, lanes]))
                again.append(local(w_out.at[core], wdown.at[1 - down_slot(k)]))
            us, ds = up_slot(k), down_slot(k)

            def token_block(r):
                here = rows(r, TB)
                w1, w2 = wup[us].reshape(D, HALF), wdown[ds].reshape(HALF, D)
                for cut in (slice(0, 256), slice(256, HALF)):
                    hidden, slope = gelu_and_slope(nn(n[here], w1[:, cut]))
                    hid[here, cut] = hidden.astype(BF)
                    gup[here, cut] = (nt(g[here], w2[cut]) * slope).astype(BF)
                for cut in (slice(0, HALF), slice(HALF, D)):
                    if k == 0:
                        acc_r[here, cut] = nn(hid[here], w2[:, cut])
                        acc_g[here, cut] = nt(gup[here], w1[cut])
                    else:
                        acc_r[here, cut] += nn(hid[here], w2[:, cut])
                        acc_g[here, cut] += nt(gup[here], w1[cut])

            turns = 2 * ROW // TB
            pl.loop(0, turns // 2)(token_block)
            advance(k, "mid")
            pl.loop(turns // 2, turns)(token_block)
            if last:
                pl.semaphore_signal(free_sem, inc=1, device_id=L.sibling(), device_id_type=MESH)
                tok_again = local(tokens, n.at[own])
            advance(k, "tokens")
            slot = (k + 2) % SLOTS
            if k >= SLOTS:
                FG[k - SLOTS].to(3)

            @pl.loop(0, places)
            def _(p):
                ring[(slot, 0) + L.place(p)] = nn(nT[rows(p, R)], gup[...]).astype(BF)

            if last:
                again.append(local(gj_out.at[:, pl.ds(0, HALF)], gup))
            advance(k, "up")

            @pl.loop(0, places)
            def _(p):
                ring[(slot, 1) + L.place(p)] = nn(gT[rows(p, R)], hid[...]).astype(BF)

            FG[k].to(0)
            advance(k, "down")

        again.append(local(heads_out, hid))
        wait_all(again)
        wo = wdown[1 - down_slot(mlp - 1)].reshape(HALF, D)

        def attention_part(here):
            total = nt(gj[here, pl.ds(0, HALF)], wup[used_up[0]].reshape(D, HALF))
            for part in range(1, 3):
                total += nt(gj[here, pl.ds(part * HALF, HALF)], wup[used_up[part]].reshape(D, HALF))
            return nn(hid[here], wo), total

        @pl.loop(0, ROW // QB)
        def _(r):
            there = pl.ds(aligned(ROW + r * QB, QB), QB)
            out, grad = attention_part(there)
            nT[rows(r, QB), pl.ds(0, D)] = (acc_r[there] + out).astype(BF)
            nT[rows(r, QB), pl.ds(D, D)] = (acc_g[there] + grad).astype(BF)

        pl.semaphore_wait(free_sem, 1)
        start_all([swap_g, swap_r])
        advance(mlp - 1, "sibling")

        @pl.loop(0, ROW // QB)
        def _(r):
            here = rows(r, QB)
            out, grad = attention_part(here)
            acc_r[here] += out
            acc_g[here] += grad

        advance(mlp - 1, "own")
        tok_again.wait()
        swap_r.wait()
        swap_g.wait()
        sum_send[0] = jnp.zeros_like(sum_send[0])
        FB = 128

        @pl.loop(0, ROW // FB)
        def _(r):
            here = rows(r, FB)
            there = pl.ds(aligned(ROW + r * FB, FB), FB)
            x = n[here].astype(F32)
            xhat, inverse = layer_norm(x)
            n[here] = (x + acc_r[here] + n[there].astype(F32)).astype(BF)
            grad = acc_g[here] + g[there].astype(F32)
            sum_send[0, 0:1] += jnp.sum(grad * xhat, axis=0, keepdims=True)
            sum_send[0, 1:2] += jnp.sum(grad, axis=0, keepdims=True)
            scaled = grad * gain[...]
            acc_g[here] = g[here].astype(F32) + inverse * (
                scaled
                - jnp.mean(scaled, axis=-1, keepdims=True)
                - xhat * jnp.mean(scaled * xhat, axis=-1, keepdims=True)
            )

        outs = [local(n.at[own], result), local(acc_g.at[pl.ds(0, ROW)], d_tokens)]

        partners = L.pairs()
        adds = [L.copy(sum_send.at[i], sum_recv.at[i], device) for i, device in enumerate(partners)]

        def sum_step(i):
            adds[i].wait()
            sum_send[i + 1] = sum_send[i] + sum_recv[i]
            if i + 1 < len(adds):
                adds[i + 1].start()

        adds[0].start()
        sum_step(0)
        u = mlp + 1
        final = FG[mlp - 1]
        advance(mlp - 1, "fin")
        final.to(1)
        advance(mlp - 1, "fin1")
        if len(adds) > 1:
            sum_step(1)
        if len(adds) > 2:
            sum_step(2)
        final.to(2)
        for i in range(mlp - 1):
            FG[i].to(3)
        slot = u % SLOTS
        S = R // 2
        for arr in range(2):
            for keep in range(2):
                lo = pl.ds(aligned((core if keep else 1 - core) * S, S), S)
                total = ring[(slot, arr) + my + (lo,)].astype(F32)
                for i in range(mlp - 1):
                    total = total + zf[i, arr, lo].astype(F32)
                if keep:
                    acc_r[arr * ROW : arr * ROW + S, half_cols] = total
                else:
                    swap_out[arr] = total.astype(BF)
        last_swap = L.copy(swap_out, swap_in, L.sibling())
        last_swap.start()
        for i in range(3, len(adds)):
            sum_step(i)
        sums_out[...] = sum_send[len(adds)]
        U[0].to(7)
        U[1].to(7)
        last_swap.wait()
        other_cols = pl.ds(aligned((1 - core) * HALF, HALF), HALF)
        for arr, ref in enumerate((d_up, d_down)):
            acc_r[arr * ROW : arr * ROW + S, other_cols] = swap_in[arr].astype(F32)
            outs.append(local(acc_r.at[pl.ds(arr * ROW, S)], ref))
        wait_all(outs)

    pl.run_scoped(feed_forward, V((2 * ROW, D), F32), V((2 * ROW, D), F32))


CB = 128


def convert_kernel(mine, theirs, res_in, tok_in, sums, up_in, down_in, d_qkv, d_out, result, d_tokens, d_gain, d_bias, d_up, d_down):
    core = lax.rem(lax.axis_index("dp"), 2)
    result[...] = res_in[...]
    d_tokens[...] = tok_in[...]
    for who, ref in ((core, mine), (1 - core, theirs)):
        for u in range(2):
            lane = who * HALF + u * 256
            for part in range(3):
                at = (part % 2) * 256
                d_qkv[:, pl.ds(aligned(part * D + lane, 256), 256)] = ref[u, part // 2, :, at : at + 256].astype(F32)
            d_out[pl.ds(aligned(lane, 256), 256)] = jnp.transpose(ref[u, 1, :, 256:].astype(F32))

    @pl.when(pl.program_id(0) == 0)
    def _():
        d_gain[...] = sums[0:1]
        d_bias[...] = sums[1:2]
        d_up[...] = up_in[...]
        if d_down.shape == down_in.shape:
            d_down[...] = down_in[...]
        else:
            d_down[...] = jnp.transpose(down_in[...])


def convert(mine, theirs, *rest):
    S = jax.ShapeDtypeStruct
    block = pl.BlockSpec((2, 2, CB, HALF), lambda r: (0, 0, r, 0))
    rows_of = pl.BlockSpec((CB, D), lambda r: (r, 0))
    whole = lambda *s: pl.BlockSpec(s, lambda r: (0, 0))
    size = rest[3].shape[0]
    turned = (D, size) if size % 128 == 0 else (size, D)
    *outs, d_down = pl.pallas_call(
        convert_kernel,
        grid=(D // CB,),
        out_shape=[
            S((D, 3 * D), F32), S((D, D), F32), S((ROW, D), BF), S((ROW, D), F32),
            S((1, D), F32), S((1, D), F32), S((size, D), F32), S(turned, F32),
        ],
        in_specs=[block, block, rows_of, rows_of, whole(8, D), whole(size, D), whole(size, D)],
        out_specs=[
            pl.BlockSpec((CB, 3 * D), lambda r: (r, 0)), pl.BlockSpec((D, CB), lambda r: (0, r)), rows_of, rows_of,
            whole(1, D), whole(1, D), whole(size, D), whole(*turned),
        ],
        cost_estimate=pl.CostEstimate(flops=10**7, bytes_accessed=36 * MiB, transcendentals=0),
        compiler_params=pltpu.CompilerParams(vmem_limit_bytes=63 * MiB),
        name="convert",
    )(mine, theirs, *rest)
    return (*outs, d_down if turned == (D, size) else d_down.T)


def shards(dp, mlp, tokens, gain, bias, w_qkv, w_out, w_up, w_down, lengths, grad_out):
    nb = (dp // 2).bit_length() - 1
    places = 1 << nb
    bits, R, Rd = (2,) * nb, D // places, HALF // places
    slots = 3
    rates = jnp.exp(jnp.arange(8).astype(F32) * (-2.0 * math.log(10000.0) / 16)).reshape(8, 1)
    anyspec, vm = pl.BlockSpec(memory_space=pl.ANY), pl.BlockSpec(memory_space=pltpu.VMEM)
    S = jax.ShapeDtypeStruct
    V = pltpu.VMEM
    two = 2 * ROW
    steps = nb + mlp.bit_length()
    gathered = (2, 2) + bits + (R, HALF)
    out_shape = [
        S((ROW, D), BF), S((ROW, D), F32), S((8, D), F32), S((R // 2, D), F32), S((R // 2, D), F32),
        S(gathered, BF), S(gathered, BF), S((mlp,) + bits + (R, HALF), BF), S((mlp,) + bits + (Rd, D), BF),
        S((two, HALF), BF), S((two, 3 * HALF), BF),
    ]
    out_specs = [anyspec] * 11
    out_specs[2] = vm
    outs = pl.pallas_call(
        functools.partial(whole_kernel, dp, mlp),
        out_shape=out_shape,
        in_specs=[anyspec, vm, vm, vm] + [anyspec] * 6,
        out_specs=out_specs,
        scratch_shapes=[
            V((two, D), BF), V((D, two), BF), V((two, D), BF), V((D, two), BF),
            V((4,) + bits + (R, HALF), BF), V((2,) + bits + (Rd, D), BF),
            V((slots, 2) + bits + (R, HALF), BF),
            [V((2, 2) + (2,) * (nb - 1 - j) + (R, HALF), BF) for j in range(nb)],
            V((2, mlp - 1, 2, R, HALF // mlp), BF), V((2, 2, R, HALF // mlp), BF), V((mlp - 1, 2, R, HALF), BF),
            V((2, R // 2, HALF), BF), V((2, R // 2, HALF), BF),
            V((2, 8, 128), jnp.int32), V((steps + 1, 8, D), F32), V((steps, 8, D), F32),
            V((two, HALF), BF), V((two, 3 * HALF), BF),
            pltpu.SemaphoreType.DMA((192,)), pltpu.SemaphoreType.DMA((192,)), pltpu.SemaphoreType.DMA((64,)),
            pltpu.SemaphoreType.REGULAR,
        ],
        compiler_params=pltpu.CompilerParams(vmem_limit_bytes=64 * MiB - (128 << 10), collective_id=0, has_side_effects=True),
        cost_estimate=pl.CostEstimate(flops=120 * 10**9, bytes_accessed=60 * MiB, transcendentals=0),
        name="block",
    )(
        jnp.pad(lengths, ((0, 7), (0, 120))), rates, gain.reshape(1, D), bias.reshape(1, D), tokens, grad_out,
        w_qkv.reshape(bits + (R, 3 * D)), w_out.reshape((2,) + bits + (Rd, D)),
        w_up.reshape(bits + (R, D)), w_down.reshape((2,) + bits + (Rd, D)),
    )
    result, d_tokens, sums, d_up, d_down, mine, theirs = outs[:7]
    d_qkv, d_out, result, d_tokens, d_gain, d_bias, d_up, d_down = convert(
        mine.reshape(2, 2, D, HALF), theirs.reshape(2, 2, D, HALF), result, d_tokens, sums, d_up, d_down
    )
    return (result, d_tokens, d_gain.reshape(D), d_bias.reshape(D), d_qkv, d_out, d_up, d_down)


def solution(mesh):
    dp, mlp = mesh.shape["dp"], mesh.shape["mlp"]
    rows_in = P(("dp", "mlp"), None)
    in_specs = (rows_in, P(), P(), P(), P(), P(None, "mlp"), P("mlp", None), rows_in, rows_in)
    out_specs = (rows_in, rows_in, P(), P(), P(), P(), P("dp", "mlp"), P("mlp", "dp"))
    body = functools.partial(shards, dp, mlp)
    return jax.shard_map(body, mesh=mesh, in_specs=in_specs, out_specs=out_specs, check_vma=False)
```

```python
import functools
import math

import jax
import jax.numpy as jnp
from jax import lax
from jax.experimental import pallas as pl
from jax.experimental.pallas import tpu as pltpu
from jax.sharding import PartitionSpec as P

D = 1024
HD = 64
ROW = 1024
EPSILON = 1e-05
ROOT_HALF = 0.7071067811865476
NORMAL_PEAK = 0.3989422804014327
BF = jnp.bfloat16
F32 = jnp.float32
QB = 256
HALF = D // 2
MiB = 1 << 20
MESH = pl.DeviceIdType.MESH


def nn(a, b):
    return lax.dot_general(a, b, (((1,), (0,)), ((), ())), preferred_element_type=F32)


def nt(a, b):
    return lax.dot_general(a, b, (((1,), (1,)), ((), ())), preferred_element_type=F32)


def tn(a, b):
    return lax.dot_general(a, b, (((0,), (0,)), ((), ())), preferred_element_type=F32)


def layer_norm(x):
    mean = jnp.mean(x, axis=-1, keepdims=True)
    centered = x - mean
    var = jnp.mean(centered * centered, axis=-1, keepdims=True)
    inverse = lax.rsqrt(var + EPSILON)
    return centered * inverse, inverse


def doc_start(lengths, row, places):
    start = jnp.zeros_like(places)
    end = jnp.zeros((1, 1), jnp.int32)
    for d in range(8):
        end = end + lengths[row, 0:1, d : d + 1]
        start = jnp.where(places >= end, end, start)
    return start


def rotary_tables(lengths, row, rates):
    places = lax.broadcasted_iota(jnp.int32, (8, ROW), 1)
    pos = places - doc_start(lengths, row, places)
    angles = pos.astype(F32) * rates
    cosine, sine = jnp.cos(angles), jnp.sin(angles)
    ones, zeros = jnp.ones((48, ROW), F32), jnp.zeros((8, ROW), F32)
    pad = jnp.zeros((48, ROW), F32)
    table = lambda *parts: jnp.transpose(jnp.concatenate(parts * 2, axis=0))
    return (
        table(cosine, cosine, ones),
        table(-sine, zeros, pad),
        table(zeros, sine, pad),
    )


def rotate(x, cosine, sine_a, sine_b):
    return x * cosine + pltpu.roll(x, 120, 1) * sine_a + pltpu.roll(x, 8, 1) * sine_b


def rotate_back(x, cosine, sine_a, sine_b):
    return x * cosine - pltpu.roll(x, 120, 1) * sine_a - pltpu.roll(x, 8, 1) * sine_b


def band(i):
    return max(0, i - 2) * QB, (i + 1) * QB


MASK_AT = [sum(band(k)[1] - band(k)[0] for k in range(i)) for i in range(5)]


ERFC_RATE = 0.55 * ROOT_HALF
ERFC_TERMS = (
    0.30159098847742044, 0.3907933818624623, -0.04130162875264046,
    0.7595567015262069, -0.5179392414738552, 0.10729981475108823,
)


def gelu_and_slope(u):
    density = jnp.exp(-0.5 * u * u)
    t = pltpu.reciprocal(1.0 + ERFC_RATE * jnp.abs(u))
    poly = 0.5 * ERFC_TERMS[5]
    for term in ERFC_TERMS[4::-1]:
        poly = poly * t + 0.5 * term
    tail = poly * t * density
    bell = jnp.where(u < 0.0, tail, 1.0 - tail)
    return u * bell, bell + u * density * NORMAL_PEAK


def aligned(start, unit):
    return pl.multiple_of(start, unit)


def rows(r, size):
    return pl.ds(aligned(r * size, size), size)
STEP_PLAN = {
    (0, False): (("W1", 1), ("W2", 0),),
    (1, False): (("W1", 2),),
    (2, True): (("W2", 1),),
    (3, False): (("W2", 2),),
    (3, True): (("U0", 0), ("W3", 0),),
    (5, False): (("W3", 1),),
    (5, True): (("U0", 1),),
    (6, True): (("W1", 3), ("W3", 2),),
    (7, False): (("U0", 2),),
    (7, True): (("U1", 0), ("W2", 3),),
}
SLICE_PLAN = {
    (0, "mid"): (("U0", 3), ("U1", 1),),
    (0, "tokens"): (("U0", 4),),
    (0, "up"): (("U1", 2),),
    (0, "down"): (("U0", 5),),
    (1, "tokens"): (("F0", 1),),
    (1, "down"): (("U1", 3), ("U1", 4),),
    (2, "mid"): (("F0", 2), ("F1", 1),),
    (2, "tokens"): (("U1", 5),),
    (2, "down"): (("U0", 6),),
    (3, "mid"): (("F1", 2),),
    (3, "up"): (("U1", 6),),
    (3, "down"): (("F2", 1), ("W3", 3),),
    (3, "sibling"): (("F2", 2),),
    (3, "own"): (("F3", 1),),
}


class Links:
    def __init__(self, dp, mlp, send_sems, recv_sems):
        self.nb, self.mlp = (dp // 2).bit_length() - 1, mlp
        self.d, self.z = lax.axis_index("dp"), lax.axis_index("mlp")
        self.core = lax.rem(self.d, 2)
        self.bits = [self.bit(self.d, 2 << (self.nb - 1 - i)) for i in range(self.nb)]
        self.send_sems, self.recv_sems, self.count = send_sems, recv_sems, 0

    @staticmethod
    def bit(index, weight):
        return lax.rem(index // weight, 2)

    def flip(self, index, weight):
        return index + weight * (1 - 2 * self.bit(index, weight))

    def sibling(self):
        return (self.flip(self.d, 1), self.z)

    def plane(self, i):
        return (self.flip(self.d, 2 << (self.nb - 1 - i)), self.z)

    def along(self, offset):
        return (self.d, lax.rem(self.z + offset, self.mlp))

    def pairs(self):
        out = [self.sibling()] + [self.plane(i) for i in range(self.nb)]
        return out + [(self.d, self.flip(self.z, 1 << b)) for b in range(self.mlp.bit_length() - 1)]

    def copy(self, src, dst, device):
        k, self.count = self.count, self.count + 1
        return pltpu.make_async_remote_copy(
            src_ref=src,
            dst_ref=dst,
            send_sem=self.send_sems.at[k],
            recv_sem=self.recv_sems.at[k],
            device_id=device,
            device_id_type=MESH,
        )

    def order(self, arr):
        return list(range(self.nb)) if arr == 0 else list(range(self.nb))[::-1]

    def at(self, done, current, value):
        out = [slice(None)] * self.nb
        for i in done:
            out[i] = self.bits[i]
        if current is not None:
            out[current] = value
        return tuple(out)

    def place(self, p):
        return tuple(lax.rem(p // (1 << (self.nb - 1 - i)), 2) for i in range(self.nb))

    def mine(self):
        return tuple(self.bits)


def start_all(copies):
    for copy in copies:
        copy.start()
    return copies


def start_split(core, copies):
    @pl.when(core == 0)
    def _():
        start_all(copies)

    @pl.when(core == 1)
    def _():
        start_all(copies[::-1])


def wait_all(copies):
    for copy in copies:
        copy.wait()


class Chain:
    def __init__(self, begin, end, marks):
        self.begin, self.end, self.marks, self.at = begin, end, marks, -1

    def run(self, at, goal):
        while at < goal:
            if at >= 0:
                self.end[at]()
            at += 1
            if at < len(self.begin):
                self.begin[at]()

    def to(self, mark):
        at, self.at = self.at, max(self.at, self.marks[mark])
        self.run(at, self.at)


class Booking:
    def __init__(self):
        self.events = {}

    def book(self, event, chain, mark):
        goal = chain.marks[mark]
        if goal > chain.at:
            self.events.setdefault(event, []).append((chain, chain.at, goal))
            chain.at = goal

    def play(self, *event):
        for chain, at, goal in self.events.get(event, ()):
            chain.run(at, goal)


def whole_kernel(
    dp, mlp,
    len_own, rates, gain, bias, tokens, grad_out, w_qkv, w_out, w_up, w_down,
    result, d_tokens, sums_out, d_up, d_down, G, Gs, up_all, down_all, heads_out, gj_out,
    n, nT, g, gT, wup, wdown, ring, recv, zr, fin, zf, swap_out, swap_in, lens, sum_send, sum_recv,
    hid, gj,
    send_sems, recv_sems, sems, free_sem,
):
    L = Links(dp, mlp, send_sems, recv_sems)
    nb, core, z = L.nb, L.core, L.z
    places = 1 << nb
    R = D // places

    barrier = pltpu.get_barrier_semaphore()
    greeted = [L.sibling()] + [L.plane(i) for i in range(nb)] + [L.along(o) for o in range(1, mlp)]
    for device in greeted:
        pl.semaphore_signal(barrier, inc=1, device_id=device, device_id_type=MESH)
    pl.semaphore_wait(barrier, len(greeted))

    used = [0]

    def make(src, dst):
        k, used[0] = used[0], used[0] + 1
        return pltpu.make_async_copy(src, dst, sems.at[k])

    def local(src, dst):
        copy = make(src, dst)
        copy.start()
        return copy

    own, sib = pl.ds(0, ROW), pl.ds(ROW, ROW)
    half_cols = pl.ds(aligned(core * HALF, HALF), HALF)
    every = (slice(None),) * nb

    len_swap = L.copy(len_own, lens.at[1], L.sibling())
    tok_swap = L.copy(tokens, n.at[sib], L.sibling())
    g_swap = L.copy(grad_out, g.at[sib], L.sibling())
    start_all([len_swap, tok_swap])
    tok_load = local(tokens, n.at[own])
    len_load = local(len_own, lens.at[0])
    g_swap.start()
    g_load = local(grad_out, g.at[own])
    w_loads = []
    for part in range(3):
        cols = pl.ds(aligned(part * D + core * HALF, HALF), HALF)
        w_loads.append(local(w_qkv.at[every + (slice(None), cols)], wup.at[part]))
    w_loads.append(local(w_out.at[core], wdown.at[0]))

    my = L.mine()

    def gather(o):
        there = lax.rem(z + o, mlp)
        stages = [
            [
                L.copy(w_up.at[my + (slice(None), half_cols)], up_all.at[(z,) + my], L.along(mlp - o)),
                L.copy(w_down.at[(core,) + my], down_all.at[(z,) + my], L.along(mlp - o)),
            ]
        ]
        for j in reversed(range(nb)):
            copies = []
            for arr, ref in enumerate((up_all, down_all)):
                order = L.order(arr)
                view = ref.at[(there,) + L.at(order[: j + 1], None, None)]
                copies.append(L.copy(view, view, L.plane(order[j])))
            stages.append(copies)
        marks = {0: 0, 1: 1, 2: 1 + nb // 2, 3: 1 + nb}
        return Chain(
            [functools.partial(start_all, stages[0])] + [functools.partial(start_split, core, s) for s in stages[1:]],
            [functools.partial(wait_all, s) for s in stages],
            marks,
        )

    slice_chain = [None] + [gather(o) for o in range(1, mlp)]

    UNITS = 2 + mlp
    SLOTS = ring.shape[0]

    def plane_stage(u, j):
        slot, out = u % SLOTS, []
        for arr in range(2):
            order = L.order(arr)
            here = order[j]
            src = ring.at[(slot, arr) + L.at(order[:j], here, 1 - L.bits[here])]
            out.append(L.copy(src, recv[j].at[u % 2, arr], L.plane(here)))
        return out

    stage = {(u, j): plane_stage(u, j) for u in range(UNITS) for j in range(nb)}

    def lead_indices(depth):
        out = [()]
        for _ in range(depth):
            out = [t + (b,) for t in out for b in range(2)]
        return out

    def plane_add(u, j):
        slot = u % SLOTS
        wait_all(stage[u, j])
        step = min(R, 64)
        for arr in range(2):
            order = L.order(arr)
            done = order[: j + 1]
            rest = sorted(order[j + 1 :])
            for lead in lead_indices(len(rest)):
                idx = [None] * nb
                for i in done:
                    idx[i] = L.bits[i]
                for i, b in zip(rest, lead):
                    idx[i] = b
                target = ring.at[(slot, arr) + tuple(idx)]
                source = recv[j].at[(u % 2, arr) + lead]

                @pl.loop(0, R // step)
                def _(r):
                    total = target[rows(r, step)].astype(F32) + source[rows(r, step)].astype(F32)
                    target[rows(r, step)] = total.astype(BF)

    ZC = HALF // mlp
    cols_of = lambda w: pl.ds(aligned(w * ZC, ZC), ZC)

    def z_scatter(u):
        out = []
        for arr in range(2):
            for o in range(1, mlp):
                there = lax.rem(z + o, mlp)
                src = ring.at[(u % SLOTS, arr) + my + (slice(None), cols_of(there))]
                out.append(L.copy(src, zr.at[u, o - 1, arr], L.along(o)))
        return out

    def z_gather(u):
        out = []
        for arr in range(2):
            view = G.at[(u, arr) + my + (slice(None), cols_of(z))]
            for o in range(1, mlp):
                out.append(L.copy(fin.at[u, arr], view, L.along(o)))
        return out

    def g_plane(u, j):
        out = []
        for arr in range(2):
            order = L.order(arr)
            view = G.at[(u, arr) + L.at(order[: j + 1], None, None)]
            out.append(L.copy(view, view, L.plane(order[j])))
        return out

    def attention_chain(u):
        scatter, back = z_scatter(u), z_gather(u)
        plane = [g_plane(u, j) for j in reversed(range(nb))]
        across = [L.copy(G.at[u], Gs.at[u], L.sibling())]
        kept = [make(fin.at[u, arr], G.at[(u, arr) + my + (slice(None), cols_of(z))]) for arr in range(2)]

        def z_sum():
            wait_all(scatter)
            for arr in range(2):
                total = ring[(u % SLOTS, arr) + my + (slice(None), cols_of(z))].astype(F32)
                for o in range(mlp - 1):
                    total = total + zr[u, o, arr].astype(F32)
                fin[u, arr] = total.astype(BF)

        begin = [functools.partial(start_split, core, stage[u, j]) for j in range(nb)]
        begin += [functools.partial(start_all, s) for s in (scatter, back + kept)]
        begin += [functools.partial(start_split, core, s) for s in plane] + [functools.partial(start_all, across)]
        end = [functools.partial(plane_add, u, j) for j in range(nb)] + [z_sum]
        end += [functools.partial(wait_all, s) for s in [back + kept] + plane + [across]]
        marks = {0: 0, 1: nb // 2, 2: nb, 3: nb + 1, 4: nb + 2, 5: nb + 2 + nb // 2, 6: 2 * nb + 2, 7: 2 * nb + 3}
        return Chain(begin, end, marks)

    def slice_grads_chain(k):
        u = k + 2
        begin = [functools.partial(start_split, core, stage[u, j]) for j in range(nb)]
        end = [functools.partial(plane_add, u, j) for j in range(nb)]
        if k < mlp - 1:
            sends = [L.copy(ring.at[(u % SLOTS, arr) + my], zf.at[k, arr], L.along(1 + k)) for arr in range(2)]
            begin.append(functools.partial(start_all, sends))
            end.append(functools.partial(wait_all, sends))
        return Chain(begin, end, {0: 0, 1: nb // 2, 2: nb, 3: nb + 1})

    U = [attention_chain(u) for u in range(2)]
    FG = [slice_grads_chain(k) for k in range(mlp)]
    W = slice_chain
    named = {"W": W, "U": U, "F": FG}
    booking = Booking()

    def book_plan(event, plan):
        for name, mark in plan:
            booking.book(event, named[name[0]][int(name[1])], mark)

    booking.book(("begin",), W[1], 0)
    for t in range(8):
        for late in (False, True):
            book_plan((t, late), STEP_PLAN.get((t, late), ()))
    booking.book(("slices",), W[1], 3)
    for k in range(mlp):
        if k + 1 < mlp - 1:
            booking.book((k, "begin"), W[k + 2], 3)
        for where in ("mid", "tokens", "up", "down"):
            if where == "down":
                booking.book((k, where), FG[k], 0)
            book_plan((k, where), SLICE_PLAN.get((min(k, mlp - 1), where), ()))
            if where == "tokens" and k >= SLOTS:
                booking.book((k, where), FG[k - SLOTS], 3)

    booking.play("begin")
    len_load.wait()
    tok_load.wait()

    @pl.loop(0, ROW // QB)
    def _(r):
        xhat, _ = layer_norm(n[rows(r, QB)].astype(F32))
        normed = (xhat * gain[...] + bias[...]).astype(BF)
        n[rows(r, QB)] = normed
        nT[:, rows(r, QB)] = jnp.transpose(normed)

    tok_swap.wait()

    @pl.loop(ROW // QB, 2 * ROW // QB)
    def _(r):
        xhat, _ = layer_norm(n[rows(r, QB)].astype(F32))
        normed = (xhat * gain[...] + bias[...]).astype(BF)
        n[rows(r, QB)] = normed
        nT[:, rows(r, QB)] = jnp.transpose(normed)

    g_load.wait()
    g_swap.wait()

    @pl.loop(0, 2 * ROW // QB)
    def _(r):
        gT[:, rows(r, QB)] = jnp.transpose(g[rows(r, QB)])

    len_swap.wait()
    wait_all(w_loads)
    lane_low = lax.broadcasted_iota(jnp.int32, (1, 128), 1) < HD

    heads = hid

    def group_saves(u):
        lanes = [pl.ds(part * HALF + u * 256, 256) for part in range(3)]
        return [make(gj.at[:, at], gj_out.at[:, at]) for at in lanes] + [make(hid.at[:, lanes[0]], heads_out.at[:, lanes[0]])]

    saves = [group_saves(u) for u in range(2)]

    def attention(tables, mask, qs, ks, vs, ghs, gkT, gvT):
        @pl.loop(0, 2)
        def _(row):
            for k, t in enumerate(rotary_tables(lens, row, rates[...])):
                tables[row, k] = t
            for i in range(ROW // QB):
                lo, hi = band(i)
                query = lax.broadcasted_iota(jnp.int32, (QB, 128), 0) + i * QB
                start = doc_start(lens, row, query)

                @pl.loop(0, (hi - lo) // 128)
                def _(j):
                    key = lax.broadcasted_iota(jnp.int32, (QB, 128), 1) + (lo + j * 128)
                    allowed = (key >= start) & (key <= query)
                    mask[row, :, pl.ds(aligned(MASK_AT[i] + j * 128, 128), 128)] = jnp.where(allowed, 0.0, -1e30)

        def attend(row, pair, col, halfway):
            out_cols = pl.ds(col, 128)
            gkT[...] = jnp.zeros_like(gkT)
            gvT[...] = jnp.zeros_like(gvT)
            def query_block(i, width):
                inside = rows(i, QB)
                keys = pl.ds(aligned((i + 1) * QB - width, QB), width)
                at = MASK_AT[i] if isinstance(i, int) else aligned(MASK_AT[2] + (i - 2) * width, 256)
                qb, gb = qs[pair, inside], ghs[pair, inside]
                kb, vb = ks[pair, keys], vs[pair, keys]
                hidden = mask[row, :, pl.ds(at, width)]
                stack = lambda x: jnp.concatenate(
                    [jnp.where(lane_low, x, jnp.zeros_like(x)), jnp.where(lane_low, jnp.zeros_like(x), x)]
                )
                q2, g2 = stack(qb), stack(gb)
                scores = nt(q2, kb) + jnp.concatenate([hidden, hidden])
                exponent = jnp.exp(scores - jnp.max(scores, axis=-1, keepdims=True))
                low = exponent.astype(BF)
                mixed = nn(low, jnp.concatenate([vb, jnp.ones_like(vb)], axis=1))
                inverse = 1.0 / mixed[:, 128:]
                head = mixed[:, :128] * inverse
                g2f = g2.astype(F32)
                centre = jnp.sum(g2f * head, axis=-1, keepdims=True)
                grad_raw = (exponent * (nt(g2, vb) - centre)).astype(BF)
                gq2 = nn(grad_raw, kb) * inverse
                gkT[:, keys] += tn((q2.astype(F32) * inverse).astype(BF), grad_raw)
                gvT[:, keys] += tn((g2f * inverse).astype(BF), low)
                heads_pair, gq_pair = (head[:QB], head[QB:]), (gq2[:QB], gq2[QB:])
                here = pl.ds(aligned(row * ROW + i * QB, QB), QB)
                heads[here, out_cols] = jnp.where(lane_low, *heads_pair).astype(BF)
                gq = jnp.where(lane_low, *gq_pair) * (HD**-0.5)
                t = [tables[row, k, inside] for k in range(3)]
                gj[here, out_cols] = rotate_back(gq, *t).astype(BF)

            query_block(0, QB)
            query_block(1, 2 * QB)
            halfway()

            @pl.loop(2, ROW // QB)
            def _(i):
                query_block(i, 3 * QB)

            @pl.loop(0, ROW // QB)
            def _(i):
                inside = rows(i, QB)
                here = pl.ds(aligned(row * ROW + i * QB, QB), QB)
                t = [tables[row, k, inside] for k in range(3)]
                gk = jnp.transpose(gkT[:, inside])
                gj[here, pl.ds(aligned(HALF + col, 128), 128)] = rotate_back(gk, *t).astype(BF)
                gv = jnp.transpose(gvT[:, inside])
                gj[here, pl.ds(aligned(2 * HALF + col, 128), 128)] = gv.astype(BF)

        PB = 512

        def project(group, row):
            gcol = aligned(group * 256, 256)

            @pl.loop(0, ROW // PB)
            def _(r):
                here = pl.ds(aligned(row * ROW + r * PB, PB), PB)
                inside = rows(r, PB)
                nb_, gb = n[here], g[here]
                t = [tables[row, k, inside] for k in range(3)]
                block = lambda part: wup[(part,) + every + (slice(None), pl.ds(gcol, 256))].reshape(D, 256)
                q, k, v = [nn(nb_, block(part)) for part in range(3)]
                gh = nt(gb, wout_rows(group))
                for p in range(2):
                    cut = slice(p * 128, p * 128 + 128)
                    qs[p, inside] = rotate(q[:, cut], *t).astype(BF) * jnp.asarray(HD**-0.5, BF)
                    ks[p, inside] = rotate(k[:, cut], *t).astype(BF)
                    vs[p, inside] = v[:, cut].astype(BF)
                    ghs[p, inside] = gh[:, cut].astype(BF)

        def wout_rows(group):
            return wdown[(0, group)].reshape(256, D)

        def group_grads(u):
            gcol = u * 256

            @pl.loop(0, places)
            def _(p):
                here = rows(p, R)
                idx = L.place(p)
                for part in range(3):
                    arr, at = part // 2, (part % 2) * 256
                    lo = part * HALF + gcol
                    ring[(u, arr) + idx + (slice(None), pl.ds(at, 256))] = nn(nT[here], gj[:, lo : lo + 256]).astype(BF)
                ring[(u, 1) + idx + (slice(None), pl.ds(256, 256))] = nn(gT[here], heads[:, gcol : gcol + 256]).astype(BF)

        def after(step, late):
            if late and step in (3, 7):
                start_all(saves[step // 4])
                group_grads(step // 4)
            booking.play(step, late)

        @pl.loop(0, 8)
        def _(step):
            group, row, pair = step // 4, lax.rem(step // 2, 2), lax.rem(step, 2)

            @pl.when(pair == 0)
            def _():
                project(group, row)

            def hooks(late):
                for t in range(8):
                    if STEP_PLAN.get((t, late)) or (late and t in (3, 7)):

                        @pl.when(step == t)
                        def _():
                            after(t, late)

            attend(row, pair, aligned(step // 4 * 256 + pair * 128, 128), lambda: hooks(False))
            hooks(True)

    V = pltpu.VMEM
    pl.run_scoped(
        attention,
        V((2, 3, ROW, 128), F32),
        V((2, QB, MASK_AT[4]), F32),
        *[V((2, ROW, 128), BF)] * 4,
        *[V((128, ROW), F32)] * 2,
    )

    def feed_forward(acc_r, acc_g):
        blocks, TB = 2 * ROW // QB, 512
        gup = gj.at[:, pl.ds(0, HALF)]

        up_slot = lambda k: lax.rem(k + 3, 4) if not isinstance(k, int) else (k + 3) % 4
        down_slot = lambda k: lax.rem(k + 1, 2) if not isinstance(k, int) else (k + 1) % 2

        def weights_in(k):
            if k == mlp - 1:
                return [
                    make(w_up.at[every + (slice(None), half_cols)], wup.at[up_slot(k)]),
                    make(w_down.at[core], wdown.at[down_slot(k)]),
                ]
            s = lax.rem(z + 1 + k, mlp)
            return [make(up_all.at[s], wup.at[up_slot(k)]), make(down_all.at[s], wdown.at[down_slot(k)])]

        def advance(k, where):
            if where in ("sibling", "own"):
                for name, mark in SLICE_PLAN.get((k, where), ()):
                    named[name[0]][int(name[1])].to(mark)
            else:
                booking.play(k, where)

        pending = [weights_in(k) for k in range(mlp)]
        swap_r = L.copy(nT.at[:, pl.ds(0, D)], n.at[sib], L.sibling())
        swap_g = L.copy(nT.at[:, pl.ds(D, D)], g.at[sib], L.sibling())
        used_up = [up_slot(k) for k in range(mlp - 1)]
        again = []
        for part in range(3):
            cols = pl.ds(aligned(part * D + core * HALF, HALF), HALF)
            again.append(make(w_qkv.at[every + (slice(None), cols)], wup.at[used_up[part]]))
            if part:
                lanes = pl.ds(part * HALF, HALF)
                again.append(make(gj_out.at[:, lanes], gj.at[:, lanes]))
        again.append(make(w_out.at[core], wdown.at[1 - down_slot(mlp - 1)]))
        tok_again = make(tokens, n.at[own])
        gj_first = make(gj_out.at[:, pl.ds(0, HALF)], gup)

        booking.play("slices")
        start_all(pending[0])
        for save in saves:
            wait_all(save)

        @pl.loop(0, 2 * ROW // QB)
        def _(r):
            acc_r[rows(r, QB)] = jnp.zeros((QB, D), F32)
            acc_g[rows(r, QB)] = jnp.zeros((QB, D), F32)

        def before_tokens(k):
            wait_all(pending[k])
            if k + 1 < mlp:
                booking.play(k, "begin")
                start_all(pending[k + 1])
            else:
                start_all(again)

        def after_tokens(k):
            if k == mlp - 1:
                pl.semaphore_signal(free_sem, inc=1, device_id=L.sibling(), device_id_type=MESH)
                tok_again.start()
            advance(k, "tokens")

        def between_grads(k):
            if k == mlp - 1:
                gj_first.start()
            advance(k, "up")

        def after_grads(k):
            advance(k, "down")

        def on_slice(k, action):
            for t in range(mlp):

                @pl.when(k == t)
                def _():
                    action(t)

        turns = 2 * ROW // TB

        @pl.loop(0, mlp)
        def _(k):
            on_slice(k, before_tokens)
            us, ds, slot = up_slot(k), down_slot(k), lax.rem(k + 2, SLOTS)

            @pl.loop(0, turns)
            def _(r):
                here = rows(r, TB)
                w1, w2 = wup[us].reshape(D, HALF), wdown[ds].reshape(HALF, D)
                for cut in (slice(0, 256), slice(256, HALF)):
                    hidden, slope = gelu_and_slope(nn(n[here], w1[:, cut]))
                    hid[here, cut] = hidden.astype(BF)
                    gup[here, cut] = (nt(g[here], w2[cut]) * slope).astype(BF)
                for cut in (slice(0, HALF), slice(HALF, D)):
                    acc_r[here, cut] += nn(hid[here], w2[:, cut])
                    acc_g[here, cut] += nt(gup[here], w1[cut])

                @pl.when(r == turns // 2 - 1)
                def _():
                    on_slice(k, lambda t: advance(t, "mid"))

            on_slice(k, after_tokens)

            @pl.loop(0, places)
            def _(p):
                ring[(slot, 0) + L.place(p)] = nn(nT[rows(p, R)], gup[...]).astype(BF)

            on_slice(k, between_grads)

            @pl.loop(0, places)
            def _(p):
                ring[(slot, 1) + L.place(p)] = nn(gT[rows(p, R)], hid[...]).astype(BF)

            on_slice(k, after_grads)

        again.append(gj_first)
        again.append(local(heads_out, hid))
        wait_all(again)
        wo = wdown[1 - down_slot(mlp - 1)].reshape(HALF, D)

        def attention_part(here):
            total = nt(gj[here, pl.ds(0, HALF)], wup[used_up[0]].reshape(D, HALF))
            for part in range(1, 3):
                total += nt(gj[here, pl.ds(part * HALF, HALF)], wup[used_up[part]].reshape(D, HALF))
            return nn(hid[here], wo), total

        @pl.loop(0, ROW // QB)
        def _(r):
            there = pl.ds(aligned(ROW + r * QB, QB), QB)
            out, grad = attention_part(there)
            nT[rows(r, QB), pl.ds(0, D)] = (acc_r[there] + out).astype(BF)
            nT[rows(r, QB), pl.ds(D, D)] = (acc_g[there] + grad).astype(BF)

        pl.semaphore_wait(free_sem, 1)
        start_all([swap_g, swap_r])
        advance(mlp - 1, "sibling")

        @pl.loop(0, ROW // QB)
        def _(r):
            here = rows(r, QB)
            out, grad = attention_part(here)
            acc_r[here] += out
            acc_g[here] += grad

        advance(mlp - 1, "own")
        tok_again.wait()
        swap_r.wait()
        swap_g.wait()
        sum_send[0] = jnp.zeros_like(sum_send[0])
        FB = 128

        @pl.loop(0, ROW // FB)
        def _(r):
            here = rows(r, FB)
            there = pl.ds(aligned(ROW + r * FB, FB), FB)
            x = n[here].astype(F32)
            xhat, inverse = layer_norm(x)
            n[here] = (x + acc_r[here] + n[there].astype(F32)).astype(BF)
            grad = acc_g[here] + g[there].astype(F32)
            sum_send[0, 0:1] += jnp.sum(grad * xhat, axis=0, keepdims=True)
            sum_send[0, 1:2] += jnp.sum(grad, axis=0, keepdims=True)
            scaled = grad * gain[...]
            acc_g[here] = g[here].astype(F32) + inverse * (
                scaled
                - jnp.mean(scaled, axis=-1, keepdims=True)
                - xhat * jnp.mean(scaled * xhat, axis=-1, keepdims=True)
            )

        outs = [local(n.at[own], result), local(acc_g.at[pl.ds(0, ROW)], d_tokens)]

        partners = L.pairs()
        adds = [L.copy(sum_send.at[i], sum_recv.at[i], device) for i, device in enumerate(partners)]

        def sum_step(i):
            adds[i].wait()
            sum_send[i + 1] = sum_send[i] + sum_recv[i]
            if i + 1 < len(adds):
                adds[i + 1].start()

        adds[0].start()
        sum_step(0)
        u = mlp + 1
        final = FG[mlp - 1]
        advance(mlp - 1, "fin")
        final.to(1)
        advance(mlp - 1, "fin1")
        if len(adds) > 1:
            sum_step(1)
        if len(adds) > 2:
            sum_step(2)
        final.to(2)
        for i in range(mlp - 1):
            FG[i].to(3)
        slot = u % SLOTS
        S = R // 2
        for arr in range(2):
            for keep in range(2):
                lo = pl.ds(aligned((core if keep else 1 - core) * S, S), S)
                total = ring[(slot, arr) + my + (lo,)].astype(F32)
                for i in range(mlp - 1):
                    total = total + zf[i, arr, lo].astype(F32)
                if keep:
                    acc_r[arr * ROW : arr * ROW + S, half_cols] = total
                else:
                    swap_out[arr] = total.astype(BF)
        last_swap = L.copy(swap_out, swap_in, L.sibling())
        last_swap.start()
        for i in range(3, len(adds)):
            sum_step(i)
        sums_out[...] = sum_send[len(adds)]
        U[0].to(7)
        U[1].to(7)
        last_swap.wait()
        other_cols = pl.ds(aligned((1 - core) * HALF, HALF), HALF)
        for arr, ref in enumerate((d_up, d_down)):
            acc_r[arr * ROW : arr * ROW + S, other_cols] = swap_in[arr].astype(F32)
            outs.append(local(acc_r.at[pl.ds(arr * ROW, S)], ref))
        wait_all(outs)

    pl.run_scoped(feed_forward, V((2 * ROW, D), F32), V((2 * ROW, D), F32))


CB = 128


def convert_kernel(mine, theirs, res_in, tok_in, sums, up_in, down_in, d_qkv, d_out, result, d_tokens, d_gain, d_bias, d_up, d_down):
    core = lax.rem(lax.axis_index("dp"), 2)
    result[...] = res_in[...]
    d_tokens[...] = tok_in[...]
    for who, ref in ((core, mine), (1 - core, theirs)):
        for u in range(2):
            lane = who * HALF + u * 256
            for part in range(3):
                at = (part % 2) * 256
                d_qkv[:, pl.ds(aligned(part * D + lane, 256), 256)] = ref[u, part // 2, :, at : at + 256].astype(F32)
            d_out[pl.ds(aligned(lane, 256), 256)] = jnp.transpose(ref[u, 1, :, 256:].astype(F32))

    @pl.when(pl.program_id(0) == 0)
    def _():
        d_gain[...] = sums[0:1]
        d_bias[...] = sums[1:2]
        d_up[...] = up_in[...]
        if d_down.shape == down_in.shape:
            d_down[...] = down_in[...]
        else:
            d_down[...] = jnp.transpose(down_in[...])


def convert(mine, theirs, *rest):
    S = jax.ShapeDtypeStruct
    block = pl.BlockSpec((2, 2, CB, HALF), lambda r: (0, 0, r, 0))
    rows_of = pl.BlockSpec((CB, D), lambda r: (r, 0))
    whole = lambda *s: pl.BlockSpec(s, lambda r: (0, 0))
    size = rest[3].shape[0]
    turned = (D, size) if size % 128 == 0 else (size, D)
    *outs, d_down = pl.pallas_call(
        convert_kernel,
        grid=(D // CB,),
        out_shape=[
            S((D, 3 * D), F32), S((D, D), F32), S((ROW, D), BF), S((ROW, D), F32),
            S((1, D), F32), S((1, D), F32), S((size, D), F32), S(turned, F32),
        ],
        in_specs=[block, block, rows_of, rows_of, whole(8, D), whole(size, D), whole(size, D)],
        out_specs=[
            pl.BlockSpec((CB, 3 * D), lambda r: (r, 0)), pl.BlockSpec((D, CB), lambda r: (0, r)), rows_of, rows_of,
            whole(1, D), whole(1, D), whole(size, D), whole(*turned),
        ],
        cost_estimate=pl.CostEstimate(flops=10**7, bytes_accessed=36 * MiB, transcendentals=0),
        compiler_params=pltpu.CompilerParams(vmem_limit_bytes=63 * MiB),
        name="convert",
    )(mine, theirs, *rest)
    return (*outs, d_down if turned == (D, size) else d_down.T)


def shards(dp, mlp, tokens, gain, bias, w_qkv, w_out, w_up, w_down, lengths, grad_out):
    nb = (dp // 2).bit_length() - 1
    places = 1 << nb
    bits, R, Rd = (2,) * nb, D // places, HALF // places
    slots = 3
    rates = jnp.exp(jnp.arange(8).astype(F32) * (-2.0 * math.log(10000.0) / 16)).reshape(8, 1)
    anyspec, vm = pl.BlockSpec(memory_space=pl.ANY), pl.BlockSpec(memory_space=pltpu.VMEM)
    S = jax.ShapeDtypeStruct
    V = pltpu.VMEM
    two = 2 * ROW
    steps = nb + mlp.bit_length()
    gathered = (2, 2) + bits + (R, HALF)
    out_shape = [
        S((ROW, D), BF), S((ROW, D), F32), S((8, D), F32), S((R // 2, D), F32), S((R // 2, D), F32),
        S(gathered, BF), S(gathered, BF), S((mlp,) + bits + (R, HALF), BF), S((mlp,) + bits + (Rd, D), BF),
        S((two, HALF), BF), S((two, 3 * HALF), BF),
    ]
    out_specs = [anyspec] * 11
    out_specs[2] = vm
    outs = pl.pallas_call(
        functools.partial(whole_kernel, dp, mlp),
        out_shape=out_shape,
        in_specs=[anyspec, vm, vm, vm] + [anyspec] * 6,
        out_specs=out_specs,
        scratch_shapes=[
            V((two, D), BF), V((D, two), BF), V((two, D), BF), V((D, two), BF),
            V((4,) + bits + (R, HALF), BF), V((2,) + bits + (Rd, D), BF),
            V((slots, 2) + bits + (R, HALF), BF),
            [V((2, 2) + (2,) * (nb - 1 - j) + (R, HALF), BF) for j in range(nb)],
            V((2, mlp - 1, 2, R, HALF // mlp), BF), V((2, 2, R, HALF // mlp), BF), V((mlp - 1, 2, R, HALF), BF),
            V((2, R // 2, HALF), BF), V((2, R // 2, HALF), BF),
            V((2, 8, 128), jnp.int32), V((steps + 1, 8, D), F32), V((steps, 8, D), F32),
            V((two, HALF), BF), V((two, 3 * HALF), BF),
            pltpu.SemaphoreType.DMA((192,)), pltpu.SemaphoreType.DMA((192,)), pltpu.SemaphoreType.DMA((64,)),
            pltpu.SemaphoreType.REGULAR,
        ],
        compiler_params=pltpu.CompilerParams(vmem_limit_bytes=64 * MiB - (128 << 10), collective_id=0, has_side_effects=True),
        cost_estimate=pl.CostEstimate(flops=120 * 10**9, bytes_accessed=60 * MiB, transcendentals=0),
        name="block",
    )(
        jnp.pad(lengths, ((0, 7), (0, 120))), rates, gain.reshape(1, D), bias.reshape(1, D), tokens, grad_out,
        w_qkv.reshape(bits + (R, 3 * D)), w_out.reshape((2,) + bits + (Rd, D)),
        w_up.reshape(bits + (R, D)), w_down.reshape((2,) + bits + (Rd, D)),
    )
    result, d_tokens, sums, d_up, d_down, mine, theirs = outs[:7]
    d_qkv, d_out, result, d_tokens, d_gain, d_bias, d_up, d_down = convert(
        mine.reshape(2, 2, D, HALF), theirs.reshape(2, 2, D, HALF), result, d_tokens, sums, d_up, d_down
    )
    return (result, d_tokens, d_gain.reshape(D), d_bias.reshape(D), d_qkv, d_out, d_up, d_down)


def solution(mesh):
    dp, mlp = mesh.shape["dp"], mesh.shape["mlp"]
    rows_in = P(("dp", "mlp"), None)
    in_specs = (rows_in, P(), P(), P(), P(), P(None, "mlp"), P("mlp", None), rows_in, rows_in)
    out_specs = (rows_in, rows_in, P(), P(), P(), P(), P("dp", "mlp"), P("mlp", "dp"))
    body = functools.partial(shards, dp, mlp)
    return jax.shard_map(body, mesh=mesh, in_specs=in_specs, out_specs=out_specs, check_vma=False)
```

```python
import functools
import math

import jax
import jax.numpy as jnp
from jax import lax
from jax.experimental import pallas as pl
from jax.experimental.pallas import tpu as pltpu
from jax.sharding import PartitionSpec as P

D = 1024
HD = 64
ROW = 1024
EPSILON = 1e-05
ROOT_HALF = 0.7071067811865476
NORMAL_PEAK = 0.3989422804014327
BF = jnp.bfloat16
F32 = jnp.float32
QB = 256
HALF = D // 2
MiB = 1 << 20
MESH = pl.DeviceIdType.MESH


def nn(a, b):
    return lax.dot_general(a, b, (((1,), (0,)), ((), ())), preferred_element_type=F32)


def nt(a, b):
    return lax.dot_general(a, b, (((1,), (1,)), ((), ())), preferred_element_type=F32)


def tn(a, b):
    return lax.dot_general(a, b, (((0,), (0,)), ((), ())), preferred_element_type=F32)


def layer_norm(x):
    mean = jnp.mean(x, axis=-1, keepdims=True)
    centered = x - mean
    var = jnp.mean(centered * centered, axis=-1, keepdims=True)
    inverse = lax.rsqrt(var + EPSILON)
    return centered * inverse, inverse


def doc_start(lengths, row, places):
    start = jnp.zeros_like(places)
    end = jnp.zeros((1, 1), jnp.int32)
    for d in range(8):
        end = end + lengths[row, 0:1, d : d + 1]
        start = jnp.where(places >= end, end, start)
    return start


def rotary_tables(lengths, row, rates):
    places = lax.broadcasted_iota(jnp.int32, (8, ROW), 1)
    pos = places - doc_start(lengths, row, places)
    angles = pos.astype(F32) * rates
    cosine, sine = jnp.cos(angles), jnp.sin(angles)
    ones, zeros = jnp.ones((48, ROW), F32), jnp.zeros((8, ROW), F32)
    pad = jnp.zeros((48, ROW), F32)
    table = lambda *parts: jnp.transpose(jnp.concatenate(parts * 2, axis=0))
    return (
        table(cosine, cosine, ones),
        table(-sine, zeros, pad),
        table(zeros, sine, pad),
    )


def rotate(x, cosine, sine_a, sine_b):
    return x * cosine + pltpu.roll(x, 120, 1) * sine_a + pltpu.roll(x, 8, 1) * sine_b


def rotate_back(x, cosine, sine_a, sine_b):
    return x * cosine - pltpu.roll(x, 120, 1) * sine_a - pltpu.roll(x, 8, 1) * sine_b


def band(i):
    return max(0, i - 2) * QB, (i + 1) * QB


MASK_AT = [sum(band(k)[1] - band(k)[0] for k in range(i)) for i in range(5)]


ERFC_RATE = 0.55 * ROOT_HALF
ERFC_TERMS = (
    0.30159098847742044, 0.3907933818624623, -0.04130162875264046,
    0.7595567015262069, -0.5179392414738552, 0.10729981475108823,
)


def gelu_and_slope(u):
    density = jnp.exp(-0.5 * u * u)
    t = pltpu.reciprocal(1.0 + ERFC_RATE * jnp.abs(u))
    poly = 0.5 * ERFC_TERMS[5]
    for term in ERFC_TERMS[4::-1]:
        poly = poly * t + 0.5 * term
    tail = poly * t * density
    bell = jnp.where(u < 0.0, tail, 1.0 - tail)
    return u * bell, bell + u * density * NORMAL_PEAK


def aligned(start, unit):
    return pl.multiple_of(start, unit)


def rows(r, size):
    return pl.ds(aligned(r * size, size), size)
STEP_PLAN = {
    (0, False): (("W1", 1), ("W2", 0),),
    (1, False): (("W1", 2),),
    (2, True): (("W2", 1),),
    (3, False): (("W2", 2),),
    (3, True): (("U0", 0), ("W3", 0),),
    (5, False): (("W3", 1),),
    (5, True): (("U0", 1),),
    (6, True): (("W1", 3), ("W3", 2),),
    (7, False): (("U0", 2),),
    (7, True): (("U1", 0), ("W2", 3),),
}
SLICE_PLAN = {
    (0, "mid"): (("U0", 3), ("U1", 1),),
    (0, "tokens"): (("U0", 4),),
    (0, "up"): (("U1", 2),),
    (0, "down"): (("U0", 5),),
    (1, "tokens"): (("F0", 1),),
    (1, "down"): (("U1", 3), ("U1", 4),),
    (2, "mid"): (("F0", 2), ("F1", 1),),
    (2, "tokens"): (("U1", 5),),
    (2, "down"): (("U0", 6),),
    (3, "mid"): (("F1", 2),),
    (3, "up"): (("U1", 6),),
    (3, "down"): (("F2", 1), ("W3", 3),),
    (3, "sibling"): (("F2", 2),),
    (3, "own"): (("F3", 1),),
}


class Links:
    def __init__(self, dp, mlp, send_sems, recv_sems):
        self.nb, self.mlp = (dp // 2).bit_length() - 1, mlp
        self.d, self.z = lax.axis_index("dp"), lax.axis_index("mlp")
        self.core = lax.rem(self.d, 2)
        self.bits = [self.bit(self.d, 2 << (self.nb - 1 - i)) for i in range(self.nb)]
        self.send_sems, self.recv_sems, self.count = send_sems, recv_sems, 0

    @staticmethod
    def bit(index, weight):
        return lax.rem(index // weight, 2)

    def flip(self, index, weight):
        return index + weight * (1 - 2 * self.bit(index, weight))

    def sibling(self):
        return (self.flip(self.d, 1), self.z)

    def plane(self, i):
        return (self.flip(self.d, 2 << (self.nb - 1 - i)), self.z)

    def along(self, offset):
        return (self.d, lax.rem(self.z + offset, self.mlp))

    def pairs(self):
        out = [self.sibling()] + [self.plane(i) for i in range(self.nb)]
        return out + [(self.d, self.flip(self.z, 1 << b)) for b in range(self.mlp.bit_length() - 1)]

    def copy(self, src, dst, device):
        k, self.count = self.count, self.count + 1
        return pltpu.make_async_remote_copy(
            src_ref=src,
            dst_ref=dst,
            send_sem=self.send_sems.at[k],
            recv_sem=self.recv_sems.at[k],
            device_id=device,
            device_id_type=MESH,
        )

    def order(self, arr):
        return list(range(self.nb)) if arr == 0 else list(range(self.nb))[::-1]

    def at(self, done, current, value):
        out = [slice(None)] * self.nb
        for i in done:
            out[i] = self.bits[i]
        if current is not None:
            out[current] = value
        return tuple(out)

    def place(self, p):
        return tuple(lax.rem(p // (1 << (self.nb - 1 - i)), 2) for i in range(self.nb))

    def mine(self):
        return tuple(self.bits)


def start_all(copies):
    for copy in copies:
        copy.start()
    return copies


def start_split(core, copies):
    @pl.when(core == 0)
    def _():
        start_all(copies)

    @pl.when(core == 1)
    def _():
        start_all(copies[::-1])


def wait_all(copies):
    for copy in copies:
        copy.wait()


class Chain:
    def __init__(self, begin, end, marks):
        self.begin, self.end, self.marks, self.at = begin, end, marks, -1

    def run(self, at, goal):
        while at < goal:
            if at >= 0:
                self.end[at]()
            at += 1
            if at < len(self.begin):
                self.begin[at]()

    def to(self, mark):
        at, self.at = self.at, max(self.at, self.marks[mark])
        self.run(at, self.at)


class Booking:
    def __init__(self):
        self.events = {}

    def book(self, event, chain, mark):
        goal = chain.marks[mark]
        if goal > chain.at:
            self.events.setdefault(event, []).append((chain, chain.at, goal))
            chain.at = goal

    def play(self, *event):
        for chain, at, goal in self.events.get(event, ()):
            chain.run(at, goal)


def whole_kernel(
    dp, mlp,
    len_own, rates, gain, bias, tokens, grad_out, w_qkv, w_out, w_up, w_down,
    result, d_tokens, sums_out, d_up, d_down, G, Gs, up_all, down_all, heads_out, gj_out,
    n, nT, g, gT, wup, wdown, ring, recv, zr, fin, zf, swap_out, swap_in, lens, sum_send, sum_recv,
    hid, gj,
    send_sems, recv_sems, sems, free_sem,
):
    L = Links(dp, mlp, send_sems, recv_sems)
    nb, core, z = L.nb, L.core, L.z
    places = 1 << nb
    R = D // places

    barrier = pltpu.get_barrier_semaphore()
    greeted = [L.sibling()] + [L.plane(i) for i in range(nb)] + [L.along(o) for o in range(1, mlp)]
    for device in greeted:
        pl.semaphore_signal(barrier, inc=1, device_id=device, device_id_type=MESH)
    pl.semaphore_wait(barrier, len(greeted))

    used = [0]

    def make(src, dst):
        k, used[0] = used[0], used[0] + 1
        return pltpu.make_async_copy(src, dst, sems.at[k])

    def local(src, dst):
        copy = make(src, dst)
        copy.start()
        return copy

    own, sib = pl.ds(0, ROW), pl.ds(ROW, ROW)
    half_cols = pl.ds(aligned(core * HALF, HALF), HALF)
    every = (slice(None),) * nb

    len_swap = L.copy(len_own, lens.at[1], L.sibling())
    tok_swap = L.copy(tokens, n.at[sib], L.sibling())
    g_swap = L.copy(grad_out, g.at[sib], L.sibling())
    start_all([len_swap, tok_swap])
    tok_load = local(tokens, n.at[own])
    len_load = local(len_own, lens.at[0])
    g_swap.start()
    g_load = local(grad_out, g.at[own])
    w_loads = []
    for part in range(3):
        cols = pl.ds(aligned(part * D + core * HALF, HALF), HALF)
        w_loads.append(local(w_qkv.at[every + (slice(None), cols)], wup.at[part]))
    w_loads.append(local(w_out.at[core], wdown.at[0]))

    my = L.mine()

    def gather(o):
        there = lax.rem(z + o, mlp)
        stages = [
            [
                L.copy(w_up.at[my + (slice(None), half_cols)], up_all.at[(z,) + my], L.along(mlp - o)),
                L.copy(w_down.at[(core,) + my], down_all.at[(z,) + my], L.along(mlp - o)),
            ]
        ]
        for j in reversed(range(nb)):
            copies = []
            for arr, ref in enumerate((up_all, down_all)):
                order = L.order(arr)
                view = ref.at[(there,) + L.at(order[: j + 1], None, None)]
                copies.append(L.copy(view, view, L.plane(order[j])))
            stages.append(copies)
        marks = {0: 0, 1: 1, 2: 1 + nb // 2, 3: 1 + nb}
        return Chain(
            [functools.partial(start_all, stages[0])] + [functools.partial(start_split, core, s) for s in stages[1:]],
            [functools.partial(wait_all, s) for s in stages],
            marks,
        )

    slice_chain = [None] + [gather(o) for o in range(1, mlp)]

    UNITS = 2 + mlp
    SLOTS = ring.shape[0]

    def plane_stage(u, j):
        slot, out = u % SLOTS, []
        for arr in range(2):
            order = L.order(arr)
            here = order[j]
            src = ring.at[(slot, arr) + L.at(order[:j], here, 1 - L.bits[here])]
            out.append(L.copy(src, recv[j].at[u % 2, arr], L.plane(here)))
        return out

    stage = {(u, j): plane_stage(u, j) for u in range(UNITS) for j in range(nb)}

    def lead_indices(depth):
        out = [()]
        for _ in range(depth):
            out = [t + (b,) for t in out for b in range(2)]
        return out

    def plane_add(u, j):
        slot = u % SLOTS
        wait_all(stage[u, j])
        step = min(R, 64)
        for arr in range(2):
            order = L.order(arr)
            done = order[: j + 1]
            rest = sorted(order[j + 1 :])
            for lead in lead_indices(len(rest)):
                idx = [None] * nb
                for i in done:
                    idx[i] = L.bits[i]
                for i, b in zip(rest, lead):
                    idx[i] = b
                target = ring.at[(slot, arr) + tuple(idx)]
                source = recv[j].at[(u % 2, arr) + lead]

                @pl.loop(0, R // step)
                def _(r):
                    total = target[rows(r, step)].astype(F32) + source[rows(r, step)].astype(F32)
                    target[rows(r, step)] = total.astype(BF)

    ZC = HALF // mlp
    cols_of = lambda w: pl.ds(aligned(w * ZC, ZC), ZC)

    def z_scatter(u):
        out = []
        for arr in range(2):
            for o in range(1, mlp):
                there = lax.rem(z + o, mlp)
                src = ring.at[(u % SLOTS, arr) + my + (slice(None), cols_of(there))]
                out.append(L.copy(src, zr.at[u, o - 1, arr], L.along(o)))
        return out

    def z_gather(u):
        out = []
        for arr in range(2):
            view = G.at[(u, arr) + my + (slice(None), cols_of(z))]
            for o in range(1, mlp):
                out.append(L.copy(fin.at[u, arr], view, L.along(o)))
        return out

    def g_plane(u, j):
        out = []
        for arr in range(2):
            order = L.order(arr)
            view = G.at[(u, arr) + L.at(order[: j + 1], None, None)]
            out.append(L.copy(view, view, L.plane(order[j])))
        return out

    def attention_chain(u):
        scatter, back = z_scatter(u), z_gather(u)
        plane = [g_plane(u, j) for j in reversed(range(nb))]
        across = [L.copy(G.at[u], Gs.at[u], L.sibling())]
        kept = [make(fin.at[u, arr], G.at[(u, arr) + my + (slice(None), cols_of(z))]) for arr in range(2)]

        def z_sum():
            wait_all(scatter)
            for arr in range(2):
                total = ring[(u % SLOTS, arr) + my + (slice(None), cols_of(z))].astype(F32)
                for o in range(mlp - 1):
                    total = total + zr[u, o, arr].astype(F32)
                fin[u, arr] = total.astype(BF)

        begin = [functools.partial(start_split, core, stage[u, j]) for j in range(nb)]
        begin += [functools.partial(start_all, s) for s in (scatter, back + kept)]
        begin += [functools.partial(start_split, core, s) for s in plane] + [functools.partial(start_all, across)]
        end = [functools.partial(plane_add, u, j) for j in range(nb)] + [z_sum]
        end += [functools.partial(wait_all, s) for s in [back + kept] + plane + [across]]
        marks = {0: 0, 1: nb // 2, 2: nb, 3: nb + 1, 4: nb + 2, 5: nb + 2 + nb // 2, 6: 2 * nb + 2, 7: 2 * nb + 3}
        return Chain(begin, end, marks)

    def slice_grads_chain(k):
        u = k + 2
        begin = [functools.partial(start_split, core, stage[u, j]) for j in range(nb)]
        end = [functools.partial(plane_add, u, j) for j in range(nb)]
        if k < mlp - 1:
            sends = [L.copy(ring.at[(u % SLOTS, arr) + my], zf.at[k, arr], L.along(1 + k)) for arr in range(2)]
            begin.append(functools.partial(start_all, sends))
            end.append(functools.partial(wait_all, sends))
        return Chain(begin, end, {0: 0, 1: nb // 2, 2: nb, 3: nb + 1})

    U = [attention_chain(u) for u in range(2)]
    FG = [slice_grads_chain(k) for k in range(mlp)]
    W = slice_chain
    named = {"W": W, "U": U, "F": FG}
    booking = Booking()

    def book_plan(event, plan):
        for name, mark in plan:
            booking.book(event, named[name[0]][int(name[1])], mark)

    booking.book(("begin",), W[1], 0)
    for t in range(8):
        for late in (False, True):
            book_plan((t, late), STEP_PLAN.get((t, late), ()))
    booking.book(("slices",), W[1], 3)
    for k in range(mlp):
        if k + 1 < mlp - 1:
            booking.book((k, "begin"), W[k + 2], 3)
        for where in ("mid", "tokens", "up", "down"):
            if where == "down":
                booking.book((k, where), FG[k], 0)
            book_plan((k, where), SLICE_PLAN.get((min(k, mlp - 1), where), ()))
            if where == "tokens" and k >= SLOTS:
                booking.book((k, where), FG[k - SLOTS], 3)

    booking.play("begin")
    len_load.wait()
    tok_load.wait()

    @pl.loop(0, ROW // QB)
    def _(r):
        xhat, _ = layer_norm(n[rows(r, QB)].astype(F32))
        normed = (xhat * gain[...] + bias[...]).astype(BF)
        n[rows(r, QB)] = normed
        nT[:, rows(r, QB)] = jnp.transpose(normed)

    tok_swap.wait()

    @pl.loop(ROW // QB, 2 * ROW // QB)
    def _(r):
        xhat, _ = layer_norm(n[rows(r, QB)].astype(F32))
        normed = (xhat * gain[...] + bias[...]).astype(BF)
        n[rows(r, QB)] = normed
        nT[:, rows(r, QB)] = jnp.transpose(normed)

    g_load.wait()
    g_swap.wait()

    @pl.loop(0, 2 * ROW // QB)
    def _(r):
        gT[:, rows(r, QB)] = jnp.transpose(g[rows(r, QB)])

    len_swap.wait()
    wait_all(w_loads)
    lane_low = lax.broadcasted_iota(jnp.int32, (1, 128), 1) < HD

    heads = hid

    def group_saves(u):
        lanes = [pl.ds(part * HALF + u * 256, 256) for part in range(3)]
        return [make(gj.at[:, at], gj_out.at[:, at]) for at in lanes] + [make(hid.at[:, lanes[0]], heads_out.at[:, lanes[0]])]

    saves = [group_saves(u) for u in range(2)]

    def attention(tables, mask, qs, ks, vs, ghs, gkT, gvT):
        @pl.loop(0, 2)
        def _(row):
            for k, t in enumerate(rotary_tables(lens, row, rates[...])):
                tables[row, k] = t
            for i in range(ROW // QB):
                lo, hi = band(i)
                query = lax.broadcasted_iota(jnp.int32, (QB, 128), 0) + i * QB
                start = doc_start(lens, row, query)

                @pl.loop(0, (hi - lo) // 128)
                def _(j):
                    key = lax.broadcasted_iota(jnp.int32, (QB, 128), 1) + (lo + j * 128)
                    allowed = (key >= start) & (key <= query)
                    mask[row, :, pl.ds(aligned(MASK_AT[i] + j * 128, 128), 128)] = jnp.where(allowed, 0.0, -1e30)

        def attend(row, pair, col, halfway):
            out_cols = pl.ds(col, 128)
            gkT[...] = jnp.zeros_like(gkT)
            gvT[...] = jnp.zeros_like(gvT)
            def query_block(i, width):
                inside = rows(i, QB)
                keys = pl.ds(aligned((i + 1) * QB - width, QB), width)
                at = MASK_AT[i] if isinstance(i, int) else aligned(MASK_AT[2] + (i - 2) * width, 256)
                qb, gb = qs[pair, inside], ghs[pair, inside]
                kb, vb = ks[pair, keys], vs[pair, keys]
                hidden = mask[row, :, pl.ds(at, width)]
                stack = lambda x: jnp.concatenate(
                    [jnp.where(lane_low, x, jnp.zeros_like(x)), jnp.where(lane_low, jnp.zeros_like(x), x)]
                )
                q2, g2 = stack(qb), stack(gb)
                scores = nt(q2, kb) + jnp.concatenate([hidden, hidden])
                exponent = jnp.exp(scores - jnp.max(scores, axis=-1, keepdims=True))
                low = exponent.astype(BF)
                mixed = nn(low, jnp.concatenate([vb, jnp.ones_like(vb)], axis=1))
                inverse = 1.0 / mixed[:, 128:]
                head = mixed[:, :128] * inverse
                g2f = g2.astype(F32)
                centre = jnp.sum(g2f * head, axis=-1, keepdims=True)
                grad_raw = (exponent * (nt(g2, vb) - centre)).astype(BF)
                gq2 = nn(grad_raw, kb) * inverse
                gkT[:, keys] += tn((q2.astype(F32) * inverse).astype(BF), grad_raw)
                gvT[:, keys] += tn((g2f * inverse).astype(BF), low)
                heads_pair, gq_pair = (head[:QB], head[QB:]), (gq2[:QB], gq2[QB:])
                here = pl.ds(aligned(row * ROW + i * QB, QB), QB)
                heads[here, out_cols] = jnp.where(lane_low, *heads_pair).astype(BF)
                gq = jnp.where(lane_low, *gq_pair) * (HD**-0.5)
                t = [tables[row, k, inside] for k in range(3)]
                gj[here, out_cols] = rotate_back(gq, *t).astype(BF)

            query_block(0, QB)
            query_block(1, 2 * QB)
            halfway()

            @pl.loop(2, ROW // QB)
            def _(i):
                query_block(i, 3 * QB)

            @pl.loop(0, ROW // QB)
            def _(i):
                inside = rows(i, QB)
                here = pl.ds(aligned(row * ROW + i * QB, QB), QB)
                t = [tables[row, k, inside] for k in range(3)]
                gk = jnp.transpose(gkT[:, inside])
                gj[here, pl.ds(aligned(HALF + col, 128), 128)] = rotate_back(gk, *t).astype(BF)
                gv = jnp.transpose(gvT[:, inside])
                gj[here, pl.ds(aligned(2 * HALF + col, 128), 128)] = gv.astype(BF)

        PB = 512

        def project(group, row):
            gcol = aligned(group * 256, 256)

            @pl.loop(0, ROW // PB)
            def _(r):
                here = pl.ds(aligned(row * ROW + r * PB, PB), PB)
                inside = rows(r, PB)
                nb_, gb = n[here], g[here]
                t = [tables[row, k, inside] for k in range(3)]
                block = lambda part: wup[(part,) + every + (slice(None), pl.ds(gcol, 256))].reshape(D, 256)
                q, k, v = [nn(nb_, block(part)) for part in range(3)]
                gh = nt(gb, wout_rows(group))
                for p in range(2):
                    cut = slice(p * 128, p * 128 + 128)
                    qs[p, inside] = rotate(q[:, cut], *t).astype(BF) * jnp.asarray(HD**-0.5, BF)
                    ks[p, inside] = rotate(k[:, cut], *t).astype(BF)
                    vs[p, inside] = v[:, cut].astype(BF)
                    ghs[p, inside] = gh[:, cut].astype(BF)

        def wout_rows(group):
            return wdown[(0, group)].reshape(256, D)

        def group_grads(u):
            gcol = u * 256

            @pl.loop(0, places)
            def _(p):
                here = rows(p, R)
                idx = L.place(p)
                for part in range(3):
                    arr, at = part // 2, (part % 2) * 256
                    lo = part * HALF + gcol
                    ring[(u, arr) + idx + (slice(None), pl.ds(at, 256))] = nn(nT[here], gj[:, lo : lo + 256]).astype(BF)
                ring[(u, 1) + idx + (slice(None), pl.ds(256, 256))] = nn(gT[here], heads[:, gcol : gcol + 256]).astype(BF)

        def after(step, late):
            if late and step in (3, 7):
                start_all(saves[step // 4])
                group_grads(step // 4)
            booking.play(step, late)

        @pl.loop(0, 8)
        def _(step):
            group, row, pair = step // 4, lax.rem(step // 2, 2), lax.rem(step, 2)

            @pl.when(pair == 0)
            def _():
                project(group, row)

            def hooks(late):
                for t in range(8):
                    if STEP_PLAN.get((t, late)) or (late and t in (3, 7)):

                        @pl.when(step == t)
                        def _():
                            after(t, late)

            attend(row, pair, aligned(step // 4 * 256 + pair * 128, 128), lambda: hooks(False))
            hooks(True)

    V = pltpu.VMEM
    pl.run_scoped(
        attention,
        V((2, 3, ROW, 128), F32),
        V((2, QB, MASK_AT[4]), F32),
        *[V((2, ROW, 128), BF)] * 4,
        *[V((128, ROW), F32)] * 2,
    )

    def feed_forward(acc_r, acc_g):
        blocks, TB = 2 * ROW // QB, 256
        gup = gj.at[:, pl.ds(0, HALF)]

        up_slot = lambda k: lax.rem(k + 3, 4) if not isinstance(k, int) else (k + 3) % 4
        down_slot = lambda k: lax.rem(k + 1, 2) if not isinstance(k, int) else (k + 1) % 2

        def weights_in(k):
            if k == mlp - 1:
                return [
                    make(w_up.at[every + (slice(None), half_cols)], wup.at[up_slot(k)]),
                    make(w_down.at[core], wdown.at[down_slot(k)]),
                ]
            s = lax.rem(z + 1 + k, mlp)
            return [make(up_all.at[s], wup.at[up_slot(k)]), make(down_all.at[s], wdown.at[down_slot(k)])]

        def advance(k, where):
            if where in ("sibling", "own"):
                for name, mark in SLICE_PLAN.get((k, where), ()):
                    named[name[0]][int(name[1])].to(mark)
            else:
                booking.play(k, where)

        pending = [weights_in(k) for k in range(mlp)]
        swap_r = L.copy(nT.at[:, pl.ds(0, D)], n.at[sib], L.sibling())
        swap_g = L.copy(nT.at[:, pl.ds(D, D)], g.at[sib], L.sibling())
        used_up = [up_slot(k) for k in range(mlp - 1)]
        again = []
        for part in range(3):
            cols = pl.ds(aligned(part * D + core * HALF, HALF), HALF)
            again.append(make(w_qkv.at[every + (slice(None), cols)], wup.at[used_up[part]]))
            if part:
                lanes = pl.ds(part * HALF, HALF)
                again.append(make(gj_out.at[:, lanes], gj.at[:, lanes]))
        again.append(make(w_out.at[core], wdown.at[1 - down_slot(mlp - 1)]))
        tok_again = make(tokens, n.at[own])
        gj_first = make(gj_out.at[:, pl.ds(0, HALF)], gup)

        booking.play("slices")
        start_all(pending[0])
        for save in saves:
            wait_all(save)

        @pl.loop(0, 2 * ROW // QB)
        def _(r):
            acc_r[rows(r, QB)] = jnp.zeros((QB, D), F32)
            acc_g[rows(r, QB)] = jnp.zeros((QB, D), F32)

        def before_tokens(k):
            wait_all(pending[k])
            if k + 1 < mlp:
                booking.play(k, "begin")
                start_all(pending[k + 1])
            else:
                start_all(again)

        def after_tokens(k):
            if k == mlp - 1:
                pl.semaphore_signal(free_sem, inc=1, device_id=L.sibling(), device_id_type=MESH)
                tok_again.start()
            advance(k, "tokens")

        def between_grads(k):
            if k == mlp - 1:
                gj_first.start()
            advance(k, "up")

        def after_grads(k):
            advance(k, "down")

        def on_slice(k, action):
            for t in range(mlp):

                @pl.when(k == t)
                def _():
                    action(t)

        turns = 2 * ROW // TB

        @pl.loop(0, mlp)
        def _(k):
            on_slice(k, before_tokens)
            us, ds, slot = up_slot(k), down_slot(k), lax.rem(k + 2, SLOTS)

            @pl.loop(0, turns)
            def _(r):
                here = rows(r, TB)
                w1, w2 = wup[us].reshape(D, HALF), wdown[ds].reshape(HALF, D)
                for cut in (slice(0, 256), slice(256, HALF)):
                    hidden, slope = gelu_and_slope(nn(n[here], w1[:, cut]))
                    hid[here, cut] = hidden.astype(BF)
                    gup[here, cut] = (nt(g[here], w2[cut]) * slope).astype(BF)
                for cut in (slice(0, HALF), slice(HALF, D)):
                    acc_r[here, cut] += nn(hid[here], w2[:, cut])
                    acc_g[here, cut] += nt(gup[here], w1[cut])

                @pl.when(r == turns // 2 - 1)
                def _():
                    on_slice(k, lambda t: advance(t, "mid"))

            on_slice(k, after_tokens)

            @pl.loop(0, places)
            def _(p):
                ring[(slot, 0) + L.place(p)] = nn(nT[rows(p, R)], gup[...]).astype(BF)

            on_slice(k, between_grads)

            @pl.loop(0, places)
            def _(p):
                ring[(slot, 1) + L.place(p)] = nn(gT[rows(p, R)], hid[...]).astype(BF)

            on_slice(k, after_grads)

        again.append(gj_first)
        again.append(local(heads_out, hid))
        wait_all(again)
        wo = wdown[1 - down_slot(mlp - 1)].reshape(HALF, D)

        def attention_part(here):
            total = nt(gj[here, pl.ds(0, HALF)], wup[used_up[0]].reshape(D, HALF))
            for part in range(1, 3):
                total += nt(gj[here, pl.ds(part * HALF, HALF)], wup[used_up[part]].reshape(D, HALF))
            return nn(hid[here], wo), total

        @pl.loop(0, ROW // QB)
        def _(r):
            there = pl.ds(aligned(ROW + r * QB, QB), QB)
            out, grad = attention_part(there)
            nT[rows(r, QB), pl.ds(0, D)] = (acc_r[there] + out).astype(BF)
            nT[rows(r, QB), pl.ds(D, D)] = (acc_g[there] + grad).astype(BF)

        pl.semaphore_wait(free_sem, 1)
        start_all([swap_g, swap_r])
        advance(mlp - 1, "sibling")

        @pl.loop(0, ROW // QB)
        def _(r):
            here = rows(r, QB)
            out, grad = attention_part(here)
            acc_r[here] += out
            acc_g[here] += grad

        advance(mlp - 1, "own")
        tok_again.wait()
        swap_r.wait()
        swap_g.wait()
        sum_send[0] = jnp.zeros_like(sum_send[0])
        FB = 128

        @pl.loop(0, ROW // FB)
        def _(r):
            here = rows(r, FB)
            there = pl.ds(aligned(ROW + r * FB, FB), FB)
            x = n[here].astype(F32)
            xhat, inverse = layer_norm(x)
            n[here] = (x + acc_r[here] + n[there].astype(F32)).astype(BF)
            grad = acc_g[here] + g[there].astype(F32)
            sum_send[0, 0:1] += jnp.sum(grad * xhat, axis=0, keepdims=True)
            sum_send[0, 1:2] += jnp.sum(grad, axis=0, keepdims=True)
            scaled = grad * gain[...]
            acc_g[here] = g[here].astype(F32) + inverse * (
                scaled
                - jnp.mean(scaled, axis=-1, keepdims=True)
                - xhat * jnp.mean(scaled * xhat, axis=-1, keepdims=True)
            )

        outs = [local(n.at[own], result), local(acc_g.at[pl.ds(0, ROW)], d_tokens)]

        partners = L.pairs()
        adds = [L.copy(sum_send.at[i], sum_recv.at[i], device) for i, device in enumerate(partners)]

        def sum_step(i):
            adds[i].wait()
            sum_send[i + 1] = sum_send[i] + sum_recv[i]
            if i + 1 < len(adds):
                adds[i + 1].start()

        adds[0].start()
        sum_step(0)
        u = mlp + 1
        final = FG[mlp - 1]
        advance(mlp - 1, "fin")
        final.to(1)
        advance(mlp - 1, "fin1")
        if len(adds) > 1:
            sum_step(1)
        if len(adds) > 2:
            sum_step(2)
        final.to(2)
        for i in range(mlp - 1):
            FG[i].to(3)
        slot = u % SLOTS
        S = R // 2
        for arr in range(2):
            for keep in range(2):
                lo = pl.ds(aligned((core if keep else 1 - core) * S, S), S)
                total = ring[(slot, arr) + my + (lo,)].astype(F32)
                for i in range(mlp - 1):
                    total = total + zf[i, arr, lo].astype(F32)
                if keep:
                    acc_r[arr * ROW : arr * ROW + S, half_cols] = total
                else:
                    swap_out[arr] = total.astype(BF)
        last_swap = L.copy(swap_out, swap_in, L.sibling())
        last_swap.start()
        for i in range(3, len(adds)):
            sum_step(i)
        sums_out[...] = sum_send[len(adds)]
        U[0].to(7)
        U[1].to(7)
        last_swap.wait()
        other_cols = pl.ds(aligned((1 - core) * HALF, HALF), HALF)
        for arr, ref in enumerate((d_up, d_down)):
            acc_r[arr * ROW : arr * ROW + S, other_cols] = swap_in[arr].astype(F32)
            outs.append(local(acc_r.at[pl.ds(arr * ROW, S)], ref))
        wait_all(outs)

    pl.run_scoped(feed_forward, V((2 * ROW, D), F32), V((2 * ROW, D), F32))


CB = 256


def convert_kernel(mine, theirs, res_in, tok_in, sums, up_in, down_in, d_qkv, d_out, result, d_tokens, d_gain, d_bias, d_up, d_down):
    core = lax.rem(lax.axis_index("dp"), 2)
    result[...] = res_in[...]
    d_tokens[...] = tok_in[...]
    for who, ref in ((core, mine), (1 - core, theirs)):
        for u in range(2):
            lane = who * HALF + u * 256
            for part in range(3):
                at = (part % 2) * 256
                d_qkv[:, pl.ds(aligned(part * D + lane, 256), 256)] = ref[u, part // 2, :, at : at + 256].astype(F32)
            d_out[pl.ds(aligned(lane, 256), 256)] = jnp.transpose(ref[u, 1, :, 256:].astype(F32))

    @pl.when(pl.program_id(0) == 0)
    def _():
        d_gain[...] = sums[0:1]
        d_bias[...] = sums[1:2]
        d_up[...] = up_in[...]
        if d_down.shape == down_in.shape:
            d_down[...] = down_in[...]
        else:
            d_down[...] = jnp.transpose(down_in[...])


def convert(mine, theirs, *rest):
    S = jax.ShapeDtypeStruct
    block = pl.BlockSpec((2, 2, CB, HALF), lambda r: (0, 0, r, 0))
    rows_of = pl.BlockSpec((CB, D), lambda r: (r, 0))
    whole = lambda *s: pl.BlockSpec(s, lambda r: (0, 0))
    size = rest[3].shape[0]
    turned = (D, size) if size % 128 == 0 else (size, D)
    *outs, d_down = pl.pallas_call(
        convert_kernel,
        grid=(D // CB,),
        out_shape=[
            S((D, 3 * D), F32), S((D, D), F32), S((ROW, D), BF), S((ROW, D), F32),
            S((1, D), F32), S((1, D), F32), S((size, D), F32), S(turned, F32),
        ],
        in_specs=[block, block, rows_of, rows_of, whole(8, D), whole(size, D), whole(size, D)],
        out_specs=[
            pl.BlockSpec((CB, 3 * D), lambda r: (r, 0)), pl.BlockSpec((D, CB), lambda r: (0, r)), rows_of, rows_of,
            whole(1, D), whole(1, D), whole(size, D), whole(*turned),
        ],
        cost_estimate=pl.CostEstimate(flops=10**7, bytes_accessed=36 * MiB, transcendentals=0),
        compiler_params=pltpu.CompilerParams(vmem_limit_bytes=63 * MiB),
        name="convert",
    )(mine, theirs, *rest)
    return (*outs, d_down if turned == (D, size) else d_down.T)


def shards(dp, mlp, tokens, gain, bias, w_qkv, w_out, w_up, w_down, lengths, grad_out):
    nb = (dp // 2).bit_length() - 1
    places = 1 << nb
    bits, R, Rd = (2,) * nb, D // places, HALF // places
    slots = 3
    rates = jnp.exp(jnp.arange(8).astype(F32) * (-2.0 * math.log(10000.0) / 16)).reshape(8, 1)
    anyspec, vm = pl.BlockSpec(memory_space=pl.ANY), pl.BlockSpec(memory_space=pltpu.VMEM)
    S = jax.ShapeDtypeStruct
    V = pltpu.VMEM
    two = 2 * ROW
    steps = nb + mlp.bit_length()
    gathered = (2, 2) + bits + (R, HALF)
    out_shape = [
        S((ROW, D), BF), S((ROW, D), F32), S((8, D), F32), S((R // 2, D), F32), S((R // 2, D), F32),
        S(gathered, BF), S(gathered, BF), S((mlp,) + bits + (R, HALF), BF), S((mlp,) + bits + (Rd, D), BF),
        S((two, HALF), BF), S((two, 3 * HALF), BF),
    ]
    out_specs = [anyspec] * 11
    out_specs[2] = vm
    outs = pl.pallas_call(
        functools.partial(whole_kernel, dp, mlp),
        out_shape=out_shape,
        in_specs=[anyspec, vm, vm, vm] + [anyspec] * 6,
        out_specs=out_specs,
        scratch_shapes=[
            V((two, D), BF), V((D, two), BF), V((two, D), BF), V((D, two), BF),
            V((4,) + bits + (R, HALF), BF), V((2,) + bits + (Rd, D), BF),
            V((slots, 2) + bits + (R, HALF), BF),
            [V((2, 2) + (2,) * (nb - 1 - j) + (R, HALF), BF) for j in range(nb)],
            V((2, mlp - 1, 2, R, HALF // mlp), BF), V((2, 2, R, HALF // mlp), BF), V((mlp - 1, 2, R, HALF), BF),
            V((2, R // 2, HALF), BF), V((2, R // 2, HALF), BF),
            V((2, 8, 128), jnp.int32), V((steps + 1, 8, D), F32), V((steps, 8, D), F32),
            V((two, HALF), BF), V((two, 3 * HALF), BF),
            pltpu.SemaphoreType.DMA((192,)), pltpu.SemaphoreType.DMA((192,)), pltpu.SemaphoreType.DMA((64,)),
            pltpu.SemaphoreType.REGULAR,
        ],
        compiler_params=pltpu.CompilerParams(vmem_limit_bytes=64 * MiB - (128 << 10), collective_id=0, has_side_effects=True),
        cost_estimate=pl.CostEstimate(flops=120 * 10**9, bytes_accessed=60 * MiB, transcendentals=0),
        name="block",
    )(
        jnp.pad(lengths, ((0, 7), (0, 120))), rates, gain.reshape(1, D), bias.reshape(1, D), tokens, grad_out,
        w_qkv.reshape(bits + (R, 3 * D)), w_out.reshape((2,) + bits + (Rd, D)),
        w_up.reshape(bits + (R, D)), w_down.reshape((2,) + bits + (Rd, D)),
    )
    result, d_tokens, sums, d_up, d_down, mine, theirs = outs[:7]
    d_qkv, d_out, result, d_tokens, d_gain, d_bias, d_up, d_down = convert(
        mine.reshape(2, 2, D, HALF), theirs.reshape(2, 2, D, HALF), result, d_tokens, sums, d_up, d_down
    )
    return (result, d_tokens, d_gain.reshape(D), d_bias.reshape(D), d_qkv, d_out, d_up, d_down)


def solution(mesh):
    dp, mlp = mesh.shape["dp"], mesh.shape["mlp"]
    rows_in = P(("dp", "mlp"), None)
    in_specs = (rows_in, P(), P(), P(), P(), P(None, "mlp"), P("mlp", None), rows_in, rows_in)
    out_specs = (rows_in, rows_in, P(), P(), P(), P(), P("dp", "mlp"), P("mlp", "dp"))
    body = functools.partial(shards, dp, mlp)
    return jax.shard_map(body, mesh=mesh, in_specs=in_specs, out_specs=out_specs, check_vma=False)
```
